256 devices in a mesh: dp: 8 (over y_hi, x), loop: 32 (over z, y_lo, core).
Axes of the slice: x: 4, y: 4 (y_hi: 2, y_lo: 2; y = y_hi * 2 + y_lo), z: 8, core: 2. Of those that a mesh axis runs over, the one named last changes fastest.
Arguments:
- tokens: bfloat16 [8, 16384, 1536], P('dp', 'loop'), may hold values from -6 to 6
- weights: bfloat16 [1536, 2304], replicated, may hold values from -2 to 2
- cotangent: bfloat16 [8, 16384, 768], P('dp', 'loop'), may hold values from -6 to 6
- token_types: int32 [8, 16384], P('dp'), may hold values from 0 to 1
- incidence: int32 [8, 256, 3], P('dp', 'loop'), may hold values 0 or 1
- window_reach: int32 [8, 256], P('dp', 'loop'), may hold values from 32 to 64, as said below
Outputs:
- attended: bfloat16 [8, 16384, 768], P('dp', 'loop')
- token_grad: bfloat16 [8, 16384, 1536], P('dp', 'loop')
- weight_grad: float32 [1536, 2304], P(('dp', 'loop'))
The draws below stay inside these ranges and needn't reach their ends.
Inputs may be any that keep to these rules, and one draw needn't show every extreme that they name: `token_types`: 0 marks a vertex token, 1 a face token. `incidence`: entry r of a query block is 1 where that block's tokens touch the key block r - 1 blocks away along the curve. `window_reach`: equal to 64 in at least one block of every mesh.
All inputs are finite; a program needn't handle non-finite values.
Results may differ from the reference program's by a relative error of at most 0.02.
Values may be sent and summed in bfloat16 or wider, within the bound.
No kernel may reach another device: no remote copies, remote signals or barrier semaphores. Data moves between devices by JAX's collectives and lax.ppermute only.
A program may use at most 128 MiB of HBM per device.

```python
import jax
import jax.numpy as jnp
from jax import lax

D = 1536
HEADS = 12
HD = 64
TILE = 64
CAP = 20
TOK_DEV = 512
HW = 768
HALO = 64
RT = 1
MESHES = 8
SEQ = 16384
NT = 256
N_LOOP = 32


def draw_window_reach(key, part):
    key_values = jax.random.fold_in(key, 11)
    key_widest = jax.random.fold_in(key, 23)
    values = jax.random.randint(key_values, (MESHES, NT), HALO // 2, HALO + 1)
    widest = jax.random.randint(key_widest, (MESHES, 1), 0, NT)
    blocks = jnp.arange(NT, dtype=jnp.int32)[None, :]
    return jnp.where(blocks == widest, HALO, values).astype(jnp.int32)


def draw_weights(key, part):
    key_entries = jax.random.fold_in(key, 31)
    key_factor = jax.random.fold_in(key, 37)
    key_top = jax.random.fold_in(key, 41)
    entries = jax.random.truncated_normal(key_entries, -4.0, 4.0, (D, 3 * HW), jnp.float32)
    head_factor = jnp.exp(jax.random.uniform(key_factor, (HEADS,), jnp.float32, 0.0, 1.7917595))
    top_head = jax.random.randint(key_top, (), 0, HEADS)
    head_factor = jnp.where(jnp.arange(HEADS, dtype=jnp.int32) == top_head, 6.0, head_factor)
    column_factor = jnp.concatenate([jnp.repeat(head_factor, HD), jnp.ones((2 * HW,), jnp.float32)])
    values = entries * column_factor[None, :] * D ** (-0.5)
    return values.astype(jnp.bfloat16)


def place_ends(values, own_key, smallest, high):
    longest = values.shape.index(max(values.shape))
    spots = []
    for shift in (0, 1):
        where = [jax.random.randint(jax.random.fold_in(own_key, axis), (), 0, length) for axis, length in enumerate(values.shape)]
        where[longest] = (where[longest] + shift) % values.shape[longest]
        spots.append(tuple(where))
    return values.at[spots[0]].set(smallest).at[spots[1]].set(high)


def spiked(array, rng, source, target, parts, factor):
    def block_of(axis_at):
        return (jnp.arange(array.shape[axis_at]) // (array.shape[axis_at] // parts)).reshape((-1,) + (1,) * (array.ndim - 1 - axis_at))

    near = jax.random.permutation(rng, parts)[block_of(target)]
    second = (block_of(target) + parts // 2) % parts
    return jnp.where((block_of(source) == near) | (block_of(source) == second), factor * array, array)


def block_levels(own_key, dims, shards, smallest, largest):
    factor_of, own = 1.0, jax.random.fold_in(own_key, 6)
    for axis_at, blocks in shards:
        steps = jnp.exp(jax.random.uniform(jax.random.fold_in(own, axis_at), (blocks,), jnp.float32, smallest / len(shards), largest / len(shards)))
        factor_of = factor_of * jnp.repeat(steps, dims[axis_at] // blocks).reshape([-1 if axis == axis_at else 1 for axis in range(len(dims))])
    return factor_of


def centred(stream_key, dims, spread, bound, pieces=(), kind=jnp.bfloat16):
    result = spread * jax.random.normal(stream_key, dims, jnp.float32)
    if pieces:
        result = result * block_levels(stream_key, dims, pieces, -0.22, 0.18)
    return jnp.clip(result, -bound, bound).astype(kind)


def heavy_noise(stream_key, extent, spread, reach, cuts, heavy, kind=jnp.bfloat16):
    result = spread * jax.random.normal(stream_key, extent, jnp.float32)
    if cuts:
        result = result * block_levels(stream_key, extent, cuts, -0.22, 0.18)
    return jnp.clip(spiked(result, jax.random.fold_in(stream_key, 3), *heavy), -reach, reach).astype(kind)


def setup_inputs(seed: int = 0) -> dict:
    key_list = jax.random.split(jax.random.key(seed), 7)
    return {
        "tokens": heavy_noise(key_list[0], (MESHES, SEQ, D), 1.0, 6.0, ((0, 8), (1, 32)), (1, 2, 32, 2.75)),
        "weights": draw_weights(jax.random.fold_in(key_list[6], 71), 0),
        "cotangent": centred(key_list[2], (MESHES, SEQ, HW), 1.0, 6.0, ((0, 8), (1, 32))),
        "token_types": place_ends(jax.random.randint(key_list[3], (MESHES, SEQ), 0, 2), jax.random.fold_in(key_list[3], 1), 0, 1).astype(jnp.int32),
        "incidence": place_ends((jax.random.randint(key_list[4], (MESHES, NT, 2 * RT + 1), 0, 4) < 3).astype(jnp.int32), jax.random.fold_in(key_list[4], 1), 0, 1),
        "window_reach": draw_window_reach(jax.random.fold_in(key_list[6], 71), 0),
    }


def window_mask(type_query, type_key, reach_tiles, incid_tiles):
    n_query = type_query.shape[0]
    n_key = type_key.shape[0]
    query_pos = jnp.arange(n_query, dtype=jnp.int32)[:, None]
    key_pos = jnp.arange(n_key, dtype=jnp.int32)[None, :]
    distance = jnp.abs(key_pos - HALO - query_pos)
    reach_rows = jnp.repeat(reach_tiles, TILE)[:, None]
    incid_rows = jnp.repeat(incid_tiles, TILE, axis=0)
    relative = key_pos // TILE - query_pos // TILE
    linked = (relative == 0) & (incid_rows[:, 0:1] == 1)
    for column in range(1, 2 * RT + 1):
        linked = linked | ((relative == column) & (incid_rows[:, column:column + 1] == 1))
    other_kind = type_query[:, None] != type_key[None, :]
    return (distance == 0) | ((distance <= reach_rows) & other_kind & linked)


def block_terms(queries, keys_values, allowed, grad_out):
    n_query = queries.shape[0]
    n_key = keys_values.shape[0]
    score_scale = HD ** -0.5
    query_heads = queries.astype(jnp.float32).reshape(n_query, HEADS, HD)
    key_heads = keys_values[:, :HW].astype(jnp.float32).reshape(n_key, HEADS, HD)
    value_heads = keys_values[:, HW:].astype(jnp.float32).reshape(n_key, HEADS, HD)
    grad_heads = grad_out.astype(jnp.float32).reshape(n_query, HEADS, HD)
    scaled = jnp.einsum("thd,shd->hts", query_heads, key_heads) * score_scale
    capped = CAP * jnp.tanh(scaled / CAP)
    numerator = jnp.where(allowed[None], jnp.exp(capped), 0.0)
    denominator = jnp.sum(numerator, axis=2, keepdims=True)
    probabilities = numerator / denominator
    probs_low = probabilities.astype(jnp.bfloat16)
    attended = jnp.einsum("hts,shd->thd", probs_low.astype(jnp.float32), value_heads)
    attended = attended.reshape(n_query, HW).astype(jnp.bfloat16)
    grad_probs = jnp.einsum("thd,shd->hts", grad_heads, value_heads)
    row_delta = jnp.einsum("thd,thd->ht", grad_heads, attended.astype(jnp.float32).reshape(n_query, HEADS, HD))
    grad_scores = probabilities * (grad_probs - row_delta[:, :, None]) * (1.0 - (capped / CAP) ** 2)
    grad_scores = grad_scores.astype(jnp.bfloat16).astype(jnp.float32)
    grad_query = jnp.einsum("hts,shd->thd", grad_scores, key_heads) * score_scale
    grad_query = grad_query.reshape(n_query, HW).astype(jnp.bfloat16)
    grad_key = jnp.einsum("hts,thd->shd", grad_scores, query_heads).reshape(n_key, HW) * score_scale
    grad_value = jnp.einsum("hts,thd->shd", probs_low.astype(jnp.float32), grad_heads).reshape(n_key, HW)
    return attended, grad_query, jnp.concatenate([grad_key, grad_value], axis=1)


def reference(tokens, weights, cotangent, token_types, incidence, window_reach):
    tiles_dev = TOK_DEV // TILE
    span = TOK_DEV + 2 * HALO

    def one_mesh(grad_total, inputs):
        mesh_tokens, mesh_grad, mesh_types, mesh_incid, mesh_reach = inputs
        projected = jnp.dot(mesh_tokens, weights, preferred_element_type=jnp.float32)
        queries = projected[:, :HW].astype(jnp.bfloat16)
        keys_values = projected[:, HW:].astype(jnp.bfloat16)
        padded_kv = jnp.concatenate([keys_values[SEQ - HALO:], keys_values, keys_values[:HALO]], axis=0)
        padded_types = jnp.concatenate([mesh_types[SEQ - HALO:], mesh_types, mesh_types[:HALO]])

        def one_block(rim_grads, block):
            row_start = (block * TOK_DEV).astype(jnp.int32)
            tile_start = (block * tiles_dev).astype(jnp.int32)
            block_queries = lax.dynamic_slice_in_dim(queries, row_start, TOK_DEV, 0)
            block_kv = lax.dynamic_slice_in_dim(padded_kv, row_start, span, 0)
            block_grad = lax.dynamic_slice_in_dim(mesh_grad, row_start, TOK_DEV, 0)
            type_query = lax.dynamic_slice_in_dim(padded_types, row_start + HALO, TOK_DEV, 0)
            type_key = lax.dynamic_slice_in_dim(padded_types, row_start, span, 0)
            reach_tiles = lax.dynamic_slice_in_dim(mesh_reach, tile_start, tiles_dev, 0)
            incid_tiles = lax.dynamic_slice_in_dim(mesh_incid, tile_start, tiles_dev, 0)
            allowed = window_mask(type_query, type_key, reach_tiles, incid_tiles)
            attended, grad_query, grad_rims = block_terms(block_queries, block_kv, allowed, block_grad)
            current = lax.dynamic_slice_in_dim(rim_grads, row_start, span, 0)
            rim_grads = lax.dynamic_update_slice_in_dim(rim_grads, current + grad_rims, row_start, 0)
            return rim_grads, (attended, grad_query)

        rim_start = jnp.zeros((SEQ + 2 * HALO, 2 * HW), jnp.float32)
        rim_grads, (attended, grad_query) = lax.scan(one_block, rim_start, jnp.arange(N_LOOP, dtype=jnp.int32))
        attended = attended.reshape(SEQ, HW)
        grad_query = grad_query.reshape(SEQ, HW)
        grad_kv = rim_grads[HALO:HALO + SEQ]
        grad_kv = grad_kv.at[:HALO].add(rim_grads[SEQ + HALO:])
        grad_kv = grad_kv.at[SEQ - HALO:].add(rim_grads[:HALO])
        grad_all = jnp.concatenate([grad_query, grad_kv.astype(jnp.bfloat16)], axis=1)
        token_grad = jnp.dot(grad_all, weights.T, preferred_element_type=jnp.float32).astype(jnp.bfloat16)
        grad_total = grad_total + jnp.dot(mesh_tokens.T, grad_all, preferred_element_type=jnp.float32)
        return grad_total, (attended, token_grad)

    grad_start = jnp.zeros((D, 3 * HW), jnp.float32)
    grad_total, (attended, token_grad) = lax.scan(
        one_mesh, grad_start, (tokens, cotangent, token_types, incidence, window_reach))
    weight_grad = grad_total * ((MESHES * SEQ) ** -0.5)
    return attended, token_grad, weight_grad
```

```python
import functools

import jax
import jax.numpy as jnp
from jax import lax
from jax.experimental import pallas as pl
from jax.experimental.pallas import tpu as pltpu
from jax.sharding import PartitionSpec as P

HEADS = 12
HD = 64
TILE = 64
CAP = 20
HW = 768
HALO = 64
GROUPS = 3
GW = HW // GROUPS
GH = HEADS // GROUPS
ROWS = 512
EXT = ROWS + 2 * HALO
TILES = ROWS // TILE
WIN = 3 * TILE
D = 1536
HALF = D // 2
AXES = ("dp", "loop")
VMEM_LIMIT = 56 * 1024 * 1024
F32 = jnp.float32
BF16 = jnp.bfloat16

NT = (((1,), (1,)), ((), ()))
TN = (((0,), (0,)), ((), ()))
NN = (((1,), (0,)), ((), ()))


def dot(a, b, dims):
    return lax.dot_general(a, b, dims, preferred_element_type=F32)


def device_at(x, y, z, core):
    return (((y // 2 * 4 + x) * 8 + z) * 2 + y % 2) * 2 + core


def route(move):
    pairs = []
    for x in range(4):
        for y in range(4):
            for z in range(8):
                for core in range(2):
                    pairs.append((device_at(x, y, z, core), device_at(*move(x, y, z, core))))
    return pairs


TO_CORE = route(lambda x, y, z, c: (x, y, z, 1 - c))
ALONG_X = [route(lambda x, y, z, c, d=d: ((x + d) % 4, y, z, c)) for d in range(4)]
ALONG_Y = [route(lambda x, y, z, c, d=d: (x, (y + d) % 4, z, c)) for d in range(4)]
ACROSS_Z = [route(lambda x, y, z, c, m=m: (x, y, z ^ m, c)) for m in (1, 2, 4)]


def along_loop(distance):
    return [((i - distance) % 32, i) for i in range(32)]


def call(kernel, out_shape, *args, **kwargs):
    return pl.pallas_call(
        kernel,
        out_shape=out_shape,
        compiler_params=pltpu.CompilerParams(vmem_limit_bytes=VMEM_LIMIT),
        **kwargs,
    )(*args)


def whole():
    return pl.BlockSpec(memory_space=pltpu.VMEM)


def reorder_kernel(index_ref, own_ref, halo_ref, out_ref):
    features = lax.broadcasted_iota(jnp.int32, (index_ref.shape[0], D), 1)
    pick = jnp.where(features == index_ref[...], 1.0, 0.0).astype(BF16)
    out_ref[:, :ROWS] = dot(pick, own_ref[...], NT).astype(BF16)
    out_ref[:, ROWS:] = dot(pick, halo_ref[...], NT).astype(BF16)


def reorder(index, own, halo, n_rows):
    block = 256
    return call(
        reorder_kernel,
        jax.ShapeDtypeStruct((n_rows, EXT), BF16),
        index,
        own,
        halo,
        grid=(n_rows // block,),
        in_specs=[
            pl.BlockSpec((block, 1), lambda i: (i, 0)),
            pl.BlockSpec((ROWS, D), lambda i: (0, 0)),
            pl.BlockSpec((2 * HALO, D), lambda i: (0, 0)),
        ],
        out_specs=pl.BlockSpec((block, EXT), lambda i: (i, 0)),
    )


def attention_kernel(
    q_ref, k_ref, v_ref, kh_ref, vh_ref, go_ref, mask_ref, _, att_ref, grad_ref, ke, ve, dk, dv
):
    ke[:HALO] = kh_ref[:HALO]
    ke[HALO : HALO + ROWS] = k_ref[...]
    ke[HALO + ROWS :] = kh_ref[HALO:]
    ve[:HALO] = vh_ref[:HALO]
    ve[HALO : HALO + ROWS] = v_ref[...]
    ve[HALO + ROWS :] = vh_ref[HALO:]
    dk[...] = jnp.zeros_like(dk)
    dv[...] = jnp.zeros_like(dv)
    head_of_lane = lax.broadcasted_iota(jnp.int32, (TILE, GW), 1) // HD

    def spread(rows):
        zero = jnp.zeros_like(rows)
        return jnp.concatenate([jnp.where(head_of_lane == h, rows, zero) for h in range(GH)], axis=0)

    def gather(square):
        out = square[:TILE]
        for h in range(1, GH):
            out = jnp.where(head_of_lane == h, square[h * TILE : (h + 1) * TILE], out)
        return out

    def step(t, _):
        at = pl.multiple_of(t * TILE, TILE)
        rows = pl.ds(at, TILE)
        window = pl.ds(at, WIN)
        q_bd = spread(q_ref[rows, :])
        g_bd = spread(go_ref[rows, :])
        k_win = ke[window, :]
        v_win = ve[window, :]
        mask = mask_ref[pl.ds(pl.multiple_of(t * WIN, WIN), WIN), :]
        mask = jnp.concatenate([mask] * (GH // 2), axis=1)
        bent = jnp.tanh(dot(k_win, q_bd, NT) * (HD**-0.5 / CAP))
        numer = jnp.exp(bent * CAP) * mask
        probs = numer * (1.0 / jnp.sum(numer, axis=0, keepdims=True))
        low = probs.astype(BF16)
        weighted = probs * dot(v_win, g_bd, NT)
        delta = jnp.sum(weighted, axis=0, keepdims=True)
        scores = ((weighted - probs * delta) * (1.0 - bent * bent)).astype(BF16)
        dk[window, :] += dot(scores, q_bd, NN)
        dv[window, :] += dot(low, g_bd, NN)
        att_ref[rows, :] = gather(dot(low, v_win, TN)).astype(BF16)
        grad_ref[rows, :GW] = (gather(dot(scores, k_win, TN)) * HD**-0.5).astype(BF16)
        return 0

    lax.fori_loop(0, TILES, step, 0, unroll=2)
    grad_ref[ROWS:, :GW] = jnp.zeros((2 * HALO, GW), BF16)
    for col, acc, factor in ((GW, dk, HD**-0.5), (2 * GW, dv, 1.0)):
        cols = slice(col, col + GW)
        grad_ref[:ROWS, cols] = (acc[HALO : HALO + ROWS] * factor).astype(BF16)
        grad_ref[ROWS : ROWS + HALO, cols] = (acc[:HALO] * factor).astype(BF16)
        grad_ref[ROWS + HALO :, cols] = (acc[HALO + ROWS :] * factor).astype(BF16)


def attention(group, proj, halo_proj, grad_out, mask, attended):
    def cols(rows, block):
        return pl.BlockSpec((rows, GW), lambda i: (0, block))

    flops = 6 * TILES * 2 * WIN * GW * GW
    return pl.pallas_call(
        attention_kernel,
        out_shape=(
            jax.ShapeDtypeStruct((ROWS, HW), BF16),
            jax.ShapeDtypeStruct((EXT, 3 * GW), BF16),
        ),
        grid=(1,),
        in_specs=[
            cols(ROWS, group),
            cols(ROWS, GROUPS + group),
            cols(ROWS, 2 * GROUPS + group),
            cols(2 * HALO, GROUPS + group),
            cols(2 * HALO, 2 * GROUPS + group),
            cols(ROWS, group),
            pl.BlockSpec((TILES * WIN, 2 * TILE), lambda i: (0, 0)),
            pl.BlockSpec(memory_space=pl.ANY),
        ],
        out_specs=(cols(ROWS, group), pl.BlockSpec((EXT, 3 * GW), lambda i: (0, 0))),
        scratch_shapes=[
            pltpu.VMEM((EXT, GW), BF16),
            pltpu.VMEM((EXT, GW), BF16),
            pltpu.VMEM((EXT, GW), F32),
            pltpu.VMEM((EXT, GW), F32),
        ],
        input_output_aliases={7: 0},
        compiler_params=pltpu.CompilerParams(vmem_limit_bytes=VMEM_LIMIT),
        cost_estimate=pl.CostEstimate(
            flops=3 * flops, bytes_accessed=4_000_000, transcendentals=2 * TILES * WIN * GW
        ),
    )(proj, proj, proj, halo_proj, halo_proj, grad_out, mask, attended)


def weight_kernel(first, x_ref, xp_ref, g_ref, gp_ref, keep_ref, *send_refs):
    own, other = g_ref[...], gp_ref[...]
    part = HALF // 4
    for j in range(4):

        def rows(ref):
            if first == "y":
                return ref[j * part : (j + 1) * part]
            return jnp.concatenate(
                [ref[i * part + j * part // 4 : i * part + (j + 1) * part // 4] for i in range(4)], axis=0
            )

        total = dot(rows(x_ref), own, NN) + dot(rows(xp_ref), other, NN)
        if j == 0:
            keep_ref[...] = total
        else:
            send_refs[j - 1][...] = total.astype(BF16)


def weight_parts(first, x_own, x_other, g_own, g_other):
    shape = (HALF // 4, 3 * GW)
    return call(
        functools.partial(weight_kernel, first),
        (jax.ShapeDtypeStruct(shape, F32),) + (jax.ShapeDtypeStruct(shape, BF16),) * 3,
        x_own,
        x_other,
        g_own,
        g_other,
        in_specs=[whole()] * 4,
        out_specs=(whole(),) * 4,
        cost_estimate=pl.CostEstimate(
            flops=2 * HALF * 2 * EXT * 3 * GW, bytes_accessed=6_000_000, transcendentals=0
        ),
    )


def split_kernel(keep_ref, a_ref, b_ref, c_ref, out_ref, *send_refs):
    part = out_ref.shape[0]
    for j in range(4):
        rows = slice(j * part, (j + 1) * part)
        total = keep_ref[rows] + a_ref[rows].astype(F32) + b_ref[rows].astype(F32) + c_ref[rows].astype(F32)
        if j == 0:
            out_ref[...] = total
        else:
            send_refs[j - 1][...] = total.astype(BF16)


def split_sum(keep, received):
    shape = (keep.shape[0] // 4, keep.shape[1])
    return call(
        split_kernel,
        (jax.ShapeDtypeStruct(shape, F32),) + (jax.ShapeDtypeStruct(shape, BF16),) * 3,
        keep,
        *received,
        in_specs=[whole()] * 4,
        out_specs=(whole(),) * 4,
    )


def exchange(parts, routes):
    return [lax.ppermute(part, AXES, routes[d + 1]) for d, part in enumerate(parts)]


def row_order(core):
    dp, loop = lax.axis_index("dp"), lax.axis_index("loop")
    y, x = dp // 4 * 2 + loop // 2 % 2, dp % 4
    z = loop // 4
    place = jnp.arange(HALF, dtype=jnp.int32)
    spot = place // 6 % 8
    to_z = z ^ (spot // 4 + spot // 2 % 2 * 2 + spot % 2 * 4)
    to_x = (x + place // 48 % 4) % 4
    to_y = (y + place // 192) % 4
    device = (((to_y // 2 * 4 + to_x) * 8 + to_z) * 2 + to_y % 2) * 2 + core
    return device * 6 + place % 6


def make_mask(types, row_start, incidence, reach):
    seq_len = types.shape[0]
    padded = jnp.concatenate([types[seq_len - HALO :], types, types[:HALO]])
    near = lax.dynamic_slice_in_dim(padded, row_start, EXT, 0)
    type_query = near[HALO : HALO + ROWS].reshape(TILES, 1, TILE)
    blocks = near.reshape(TILES + 2, TILE)
    type_key = jnp.concatenate([blocks[o : o + TILES] for o in range(3)], axis=1)[:, :, None]
    key_pos = jnp.arange(WIN, dtype=jnp.int32)[None, :, None]
    query_pos = jnp.arange(TILE, dtype=jnp.int32)[None, None, :]
    distance = jnp.abs(key_pos - HALO - query_pos)
    linked = jnp.repeat(incidence, TILE, axis=1)[:, :, None] == 1
    allowed = (distance == 0) | (
        (distance <= reach[:, None, None]) & (type_query != type_key) & linked
    )
    mask = allowed.astype(F32)
    return jnp.concatenate([mask, mask], axis=2).reshape(TILES * WIN, 2 * TILE)


def body(tokens, weights, cotangent, token_types, incidence, window_reach):
    own = tokens[0]
    core = lax.axis_index("loop") % 2
    left = lax.ppermute(own[ROWS - HALO :], "loop", along_loop(1))
    right = lax.ppermute(own[:HALO], "loop", along_loop(-1))
    halo = jnp.concatenate([left, right], axis=0)
    proj = jnp.dot(own, weights, preferred_element_type=F32).astype(BF16)
    halo_proj = jnp.dot(halo, weights, preferred_element_type=F32).astype(BF16)
    mask = make_mask(token_types[0], lax.axis_index("loop") * ROWS, incidence[0], window_reach[0])

    x_send = reorder(row_order(1 - core)[:, None], own, halo, HALF)
    x_other = lax.ppermute(x_send, AXES, TO_CORE)
    x_own = reorder(row_order(core)[:, None], own, halo, HALF)

    attended = jnp.zeros((ROWS, HW), BF16)
    grads, parts = [], []
    for group in range(GROUPS):
        attended, grad = attention(group, proj, halo_proj, cotangent[0], mask, attended)
        grads.append(grad)
        grad_other = lax.ppermute(grad, AXES, TO_CORE)
        first = "yxy"[group]
        keep, *sent = weight_parts(first, x_own, x_other, grad, grad_other)
        received = exchange(sent, ALONG_Y if first == "y" else ALONG_X)
        keep, *sent = split_sum(keep, received)
        received = exchange(sent, ALONG_X if first == "y" else ALONG_Y)
        parts.append(keep + sum(r.astype(F32) for r in received))

    total = jnp.concatenate(parts, axis=1)
    for way in ACROSS_Z:
        half = total.shape[0] // 2
        total = total[:half] + lax.ppermute(total[half:].astype(BF16), AXES, way).astype(F32)
    total = total * (256 * ROWS) ** -0.5
    pieces = [
        total[:, g * 3 * GW + k * GW : g * 3 * GW + (k + 1) * GW] for k in range(3) for g in range(GROUPS)
    ]
    weight_grad = jnp.concatenate(pieces, axis=1)

    rim_left = jnp.concatenate([g[ROWS : ROWS + HALO, GW:] for g in grads], axis=1)
    rim_right = jnp.concatenate([g[ROWS + HALO :, GW:] for g in grads], axis=1)
    from_right = lax.ppermute(rim_left, "loop", along_loop(-1))
    from_left = lax.ppermute(rim_right, "loop", along_loop(1))

    def columns(g, k):
        cols = g_cols = grads[g][:ROWS, k * GW : (k + 1) * GW]
        if k:
            at = slice(g * 2 * GW + (k - 1) * GW, g * 2 * GW + k * GW)
            top = g_cols[:HALO].astype(F32) + from_left[:, at].astype(F32)
            low = g_cols[ROWS - HALO :].astype(F32) + from_right[:, at].astype(F32)
            cols = jnp.concatenate([top.astype(BF16), g_cols[HALO : ROWS - HALO], low.astype(BF16)], axis=0)
        return cols

    grad_all = jnp.concatenate([columns(g, k) for k in range(3) for g in range(GROUPS)], axis=1)
    token_grad = dot(grad_all, weights, NT).astype(BF16)
    return attended[None], token_grad[None], weight_grad


def solution(mesh):
    in_specs = (
        P("dp", "loop", None),
        P(),
        P("dp", "loop", None),
        P("dp", None),
        P("dp", "loop", None),
        P("dp", "loop"),
    )
    out_specs = (P("dp", "loop", None), P("dp", "loop", None), P(("dp", "loop"), None))
    return jax.shard_map(body, mesh=mesh, in_specs=in_specs, out_specs=out_specs, check_vma=False)
```

```python
import functools

import jax
import jax.numpy as jnp
from jax import lax
from jax.experimental import pallas as pl
from jax.experimental.pallas import tpu as pltpu
from jax.sharding import PartitionSpec as P

HEADS = 12
HD = 64
TILE = 64
CAP = 20
HW = 768
HALO = 64
GROUPS = 3
GW = HW // GROUPS
GH = HEADS // GROUPS
ROWS = 512
EXT = ROWS + 2 * HALO
TILES = ROWS // TILE
WIN = 3 * TILE
D = 1536
HALF = D // 2
AXES = ("dp", "loop")
MIB = 1024 * 1024
F32 = jnp.float32
BF16 = jnp.bfloat16

NT = (((1,), (1,)), ((), ()))
TN = (((0,), (0,)), ((), ()))
NN = (((1,), (0,)), ((), ()))


def dot(a, b, dims):
    return lax.dot_general(a, b, dims, preferred_element_type=F32)


def device_at(x, y, z, core):
    return (((y // 2 * 4 + x) * 8 + z) * 2 + y % 2) * 2 + core


def route(move):
    pairs = []
    for x in range(4):
        for y in range(4):
            for z in range(8):
                for core in range(2):
                    pairs.append((device_at(x, y, z, core), device_at(*move(x, y, z, core))))
    return pairs


TO_CORE = route(lambda x, y, z, c: (x, y, z, 1 - c))
ACROSS_X = [route(lambda x, y, z, c, m=m: (x ^ m, y, z, c)) for m in (1, 2, 3)]
ACROSS_Y = [route(lambda x, y, z, c, m=m: (x, y ^ m, z, c)) for m in (1, 2, 3)]
ACROSS_Z = [route(lambda x, y, z, c, m=m: (x, y, z ^ m, c)) for m in (1, 2, 4)]


def along_loop(distance):
    return [((i - distance) % 32, i) for i in range(32)]


def call(kernel, out_shape, *args, vmem=16, **kwargs):
    return pl.pallas_call(
        kernel,
        out_shape=out_shape,
        compiler_params=pltpu.CompilerParams(vmem_limit_bytes=vmem * MIB),
        **kwargs,
    )(*args)


def whole():
    return pl.BlockSpec(memory_space=pltpu.VMEM)


def scalars():
    return pl.BlockSpec(memory_space=pltpu.SMEM)


def anywhere():
    return pl.BlockSpec(memory_space=pl.ANY)


def shape(rows, cols, dtype):
    return jax.ShapeDtypeStruct((rows, cols), dtype)


def cost(flops, size, transcendentals=0):
    return pl.CostEstimate(flops=flops, bytes_accessed=size, transcendentals=transcendentals)


def mask_kernel(incidence_ref, reach_ref, types_ref, out_ref):
    row = types_ref[...].astype(F32)
    column = jnp.broadcast_to(row, (2 * TILE, EXT)).T
    key = lax.broadcasted_iota(jnp.int32, (WIN, 2 * TILE), 0)
    query = lax.broadcasted_iota(jnp.int32, (WIN, 2 * TILE), 1) % TILE
    distance = jnp.abs(key - HALO - query)
    for t in range(TILES):
        own = row[:, HALO + t * TILE : HALO + (t + 1) * TILE]
        other_kind = column[t * TILE : t * TILE + WIN] != jnp.concatenate([own, own], axis=1)
        linked = [jnp.full((TILE, 2 * TILE), incidence_ref[t, r], jnp.int32) for r in range(3)]
        linked = jnp.concatenate(linked, axis=0) == 1
        allowed = (distance == 0) | ((distance <= reach_ref[t]) & other_kind & linked)
        out_ref[t * WIN : (t + 1) * WIN, :] = jnp.where(allowed, 1.0, 0.0)


def make_mask(types, row_start, incidence, reach):
    seq_len = types.shape[1]
    padded = jnp.concatenate([types[:, seq_len - HALO :], types, types[:, :HALO]], axis=1)
    near = lax.dynamic_slice_in_dim(padded, row_start, EXT, 1)
    return call(
        mask_kernel,
        shape(TILES * WIN, 2 * TILE, F32),
        incidence,
        reach,
        near,
        in_specs=[scalars(), scalars(), whole()],
        out_specs=whole(),
    )


def projection_kernel(own_ref, left_ref, right_ref, w_ref, out_ref, rows):
    @pl.when(pl.program_id(0) == 0)
    def _():
        rows[:ROWS] = own_ref[...]
        rows[ROWS : ROWS + HALO] = left_ref[...]
        rows[ROWS + HALO :] = right_ref[...]

    out_ref[...] = dot(rows[...], w_ref[...], NN).astype(BF16)


def projection(own, left, right, weights):
    cols = weights.shape[1]
    return call(
        projection_kernel,
        shape(EXT, cols, BF16),
        own,
        left,
        right,
        weights,
        vmem=24,
        grid=(cols // GW,),
        in_specs=[
            pl.BlockSpec((ROWS, D), lambda i: (0, 0)),
            pl.BlockSpec((HALO, D), lambda i: (0, 0)),
            pl.BlockSpec((HALO, D), lambda i: (0, 0)),
            pl.BlockSpec((D, GW), lambda i: (0, i)),
        ],
        out_specs=pl.BlockSpec((EXT, GW), lambda i: (0, i)),
        scratch_shapes=[pltpu.VMEM((EXT, D), BF16)],
        cost_estimate=cost(2 * EXT * D * cols, 12_000_000),
    )


def reorder_kernel(place_ref, own_ref, left_ref, right_ref, same_ref, other_ref, rows):
    x, y, z, core = place_ref[0], place_ref[1], place_ref[2], place_ref[3]
    rows[:ROWS] = own_ref[...]
    rows[ROWS : ROWS + HALO] = left_ref[...]
    rows[ROWS + HALO :] = right_ref[...]
    block = D // 4
    half = block // 2
    place = lax.broadcasted_iota(jnp.int32, (block, block), 0)
    feature = lax.broadcasted_iota(jnp.int32, (block, block), 1)
    other = (place >= half).astype(jnp.int32)
    place = place - other * half
    low_y = (place >= half // 2).astype(jnp.int32)
    place = place - low_y * (half // 2)
    low_x = (place >= half // 4).astype(jnp.int32)
    place = place - low_x * (half // 4)
    spot = lax.shift_right_logical(place * 10923, 16)
    place = place - spot * 6
    to_z = z ^ (lax.shift_right_logical(spot, 2) + (spot & 2) + (spot & 1) * 4)
    source = (low_x ^ (x & 1)) * half + to_z * 24 + (low_y ^ (y & 1)) * 12 + (other ^ core) * 6 + place
    pick = jnp.where(feature == source, 1.0, 0.0).astype(BF16)
    piece = half // 4
    for a in range(2):
        for b in range(2):
            at = (lax.shift_right_logical(y, 1) ^ a) * 2 + (lax.shift_right_logical(x, 1) ^ b)
            cols = rows[:, pl.ds(pl.multiple_of(at * block, 128), block)]
            got = dot(pick, cols, NT).astype(BF16)
            for c, ref in enumerate((same_ref, other_ref)):
                for low in range(4):
                    jy, jx = 2 * a + low // 2, 2 * b + low % 2
                    ref[jy * half + jx * piece : jy * half + (jx + 1) * piece] = got[
                        c * half + low * piece : c * half + (low + 1) * piece
                    ]


def reorder(place, own, left, right, after):
    def kernel(place_ref, own_ref, left_ref, right_ref, _, *refs):
        reorder_kernel(place_ref, own_ref, left_ref, right_ref, *refs)

    return call(
        kernel,
        (shape(HALF, EXT, BF16),) * 2,
        place,
        own,
        left,
        right,
        after,
        in_specs=[scalars(), whole(), whole(), whole(), anywhere()],
        out_specs=(whole(),) * 2,
        scratch_shapes=[pltpu.VMEM((EXT, D), BF16)],
        cost_estimate=cost(8 * EXT * (D // 4) ** 2, 4_000_000),
    )


def attention_kernel(n_carried, q_ref, k_ref, v_ref, go_ref, mask_ref, *refs):
    att_ref, left_ref, right_ref, grad_ref, ke, ve, dk, dv = refs[n_carried:]
    for src, dst in ((k_ref, ke), (v_ref, ve)):
        dst[:HALO] = src[ROWS : ROWS + HALO]
        dst[HALO : HALO + ROWS] = src[:ROWS]
        dst[HALO + ROWS :] = src[ROWS + HALO :]
    dk[...] = jnp.zeros_like(dk)
    dv[...] = jnp.zeros_like(dv)
    head_of_lane = lax.broadcasted_iota(jnp.int32, (TILE, GW), 1) // HD

    def spread(rows):
        zero = jnp.zeros_like(rows)
        return jnp.concatenate([jnp.where(head_of_lane == h, rows, zero) for h in range(GH)], axis=0)

    def gather(square):
        out = square[:TILE]
        for h in range(1, GH):
            out = jnp.where(head_of_lane == h, square[h * TILE : (h + 1) * TILE], out)
        return out

    def step(t, _):
        at = pl.multiple_of(t * TILE, TILE)
        rows = pl.ds(at, TILE)
        window = pl.ds(at, WIN)
        q_bd = spread(q_ref[rows, :])
        g_bd = spread(go_ref[rows, :])
        k_win = ke[window, :]
        v_win = ve[window, :]
        mask = mask_ref[pl.ds(pl.multiple_of(t * WIN, WIN), WIN), :]
        mask = jnp.concatenate([mask] * (GH // 2), axis=1)
        bent = jnp.tanh(dot(k_win, q_bd, NT) * (HD**-0.5 / CAP))
        numer = jnp.exp(bent * CAP) * mask
        probs = numer * (1.0 / jnp.sum(numer, axis=0, keepdims=True))
        low = probs.astype(BF16)
        weighted = probs * dot(v_win, g_bd, NT)
        delta = jnp.sum(weighted, axis=0, keepdims=True)
        scores = ((weighted - probs * delta) * (1.0 - bent * bent)).astype(BF16)
        dk[window, :] += dot(scores, q_bd, NN)
        dv[window, :] += dot(low, g_bd, NN)
        att_ref[rows, :] = gather(dot(low, v_win, TN)).astype(BF16)
        grad_ref[rows, :GW] = (gather(dot(scores, k_win, TN)) * HD**-0.5).astype(BF16)
        return 0

    lax.fori_loop(0, TILES, step, 0, unroll=4)
    grad_ref[ROWS:, :GW] = jnp.zeros((2 * HALO, GW), BF16)
    for part, acc, factor in ((1, dk, HD**-0.5), (2, dv, 1.0)):
        cols = slice(part * GW, (part + 1) * GW)
        rim_cols = slice((part - 1) * GW, part * GW)
        left = (acc[:HALO] * factor).astype(BF16)
        right = (acc[HALO + ROWS :] * factor).astype(BF16)
        grad_ref[:ROWS, cols] = (acc[HALO : HALO + ROWS] * factor).astype(BF16)
        grad_ref[ROWS : ROWS + HALO, cols] = left
        grad_ref[ROWS + HALO :, cols] = right
        left_ref[:, rim_cols] = left
        right_ref[:, rim_cols] = right


def attention(group, proj, grad_out, mask, carried, after):
    def cols(rows, block, width=GW):
        return pl.BlockSpec((rows, width), lambda i: (0, block))

    extra = list(carried) + list(after)
    return call(
        functools.partial(attention_kernel, len(extra)),
        (shape(ROWS, HW, BF16), shape(HALO, 2 * HW, BF16), shape(HALO, 2 * HW, BF16), shape(EXT, 3 * GW, BF16)),
        proj,
        proj,
        proj,
        grad_out,
        mask,
        *extra,
        vmem=20,
        grid=(1,),
        in_specs=[
            cols(ROWS, group),
            cols(EXT, GROUPS + group),
            cols(EXT, 2 * GROUPS + group),
            cols(ROWS, group),
            pl.BlockSpec((TILES * WIN, 2 * TILE), lambda i: (0, 0)),
        ]
        + [anywhere()] * len(extra),
        out_specs=(
            cols(ROWS, group),
            cols(HALO, group, 2 * GW),
            cols(HALO, group, 2 * GW),
            pl.BlockSpec((EXT, 3 * GW), lambda i: (0, 0)),
        ),
        scratch_shapes=[
            pltpu.VMEM((EXT, GW), BF16),
            pltpu.VMEM((EXT, GW), BF16),
            pltpu.VMEM((EXT, GW), F32),
            pltpu.VMEM((EXT, GW), F32),
        ],
        input_output_aliases={5 + i: i for i in range(len(carried))},
        cost_estimate=cost(36 * TILES * WIN * GW * GW, 4_000_000, 2 * TILES * WIN * GW),
    )


def weight_kernel(first, x_ref, xp_ref, g_ref, gp_ref, _, keep_ref, *send_refs):
    total = dot(x_ref[...], g_ref[...], NN) + dot(xp_ref[...], gp_ref[...], NN)
    part = HALF // 4
    piece = part // 4
    for j in range(4):
        for i in range(4):
            jy, jx = (j, i) if first == "y" else (i, j)
            rows = total[jy * part + jx * piece : jy * part + (jx + 1) * piece]
            at = slice(i * piece, (i + 1) * piece)
            if j == 0:
                keep_ref[at] = rows
            else:
                send_refs[j - 1][at] = rows.astype(BF16)


def weight_parts(first, x_own, x_other, g_own, g_other, after):
    part = HALF // 4
    resident = pl.BlockSpec((HALF, EXT), lambda i: (0, 0))
    moving = pl.BlockSpec((EXT, GW), lambda i: (0, i))
    return call(
        functools.partial(weight_kernel, first),
        (shape(part, 3 * GW, F32),) + (shape(part, 3 * GW, BF16),) * 3,
        x_own,
        x_other,
        g_own,
        g_other,
        after,
        grid=(3,),
        in_specs=[resident, resident, moving, moving, anywhere()],
        out_specs=(pl.BlockSpec((part, GW), lambda i: (0, i)),) * 4,
        cost_estimate=cost(4 * HALF * EXT * 3 * GW, 6_000_000),
    )


def split_kernel(keep_ref, a_ref, b_ref, c_ref, out_ref, *send_refs):
    part = out_ref.shape[0]
    for j in range(4):
        rows = slice(j * part, (j + 1) * part)
        total = keep_ref[rows] + a_ref[rows].astype(F32) + b_ref[rows].astype(F32) + c_ref[rows].astype(F32)
        if j == 0:
            out_ref[...] = total
        else:
            send_refs[j - 1][...] = total.astype(BF16)


def split_sum(keep, received):
    rows, cols = keep.shape[0] // 4, keep.shape[1]
    return call(
        split_kernel,
        (shape(rows, cols, F32),) + (shape(rows, cols, BF16),) * 3,
        keep,
        *received,
        in_specs=[whole()] * 4,
        out_specs=(whole(),) * 4,
    )


def join_kernel(*refs):
    keep_ref, send_ref = refs[-2:]
    half = keep_ref.shape[0]
    for g in range(GROUPS):
        total = refs[4 * g][...]
        for r in refs[4 * g + 1 : 4 * g + 4]:
            total = total + r[...].astype(F32)
        cols = slice(g * 3 * GW, (g + 1) * 3 * GW)
        keep_ref[:, cols] = total[:half]
        send_ref[:, cols] = total[half:].astype(BF16)


def halve_kernel(keep_ref, got_ref, out_ref, send_ref):
    half = out_ref.shape[0]
    total = keep_ref[...] + got_ref[...].astype(F32)
    out_ref[...] = total[:half]
    send_ref[...] = total[half:].astype(BF16)


def last_kernel(factor, keep_ref, got_ref, out_ref):
    total = (keep_ref[...] + got_ref[...].astype(F32)) * factor
    for g in range(GROUPS):
        for k in range(3):
            at = (g * 3 + k) * GW
            out_ref[:, k * HW + g * GW : k * HW + (g + 1) * GW] = total[:, at : at + GW]


def halves(kernel, rows, *args):
    cols = 3 * HW
    return call(
        kernel,
        (shape(rows, cols, F32), shape(rows, cols, BF16)),
        *args,
        in_specs=[whole()] * len(args),
        out_specs=(whole(),) * 2,
    )


def exchange(parts, routes):
    return [lax.ppermute(part, AXES, way) for part, way in zip(parts, routes)]


def token_kernel(a_ref, b_ref, c_ref, left_ref, right_ref, w_ref, out_ref, grad):
    @pl.when(pl.program_id(0) == 0)
    def _():
        for g, ref in enumerate((a_ref, b_ref, c_ref)):
            for k in range(3):
                cols = slice(k * HW + g * GW, k * HW + (g + 1) * GW)
                own = slice(k * GW, (k + 1) * GW)
                if k == 0:
                    grad[:, cols] = ref[:ROWS, own]
                    continue
                rim = slice((2 * g + k - 1) * GW, (2 * g + k) * GW)
                for edge, got in ((slice(0, HALO), left_ref), (slice(ROWS - HALO, ROWS), right_ref)):
                    grad[edge, cols] = (ref[edge, own].astype(F32) + got[:, rim].astype(F32)).astype(BF16)
                grad[HALO : ROWS - HALO, cols] = ref[HALO : ROWS - HALO, own]

    out_ref[...] = dot(grad[...], w_ref[...], NT).astype(BF16)


def token_gradient(grads, from_left, from_right, weights):
    block = 256
    cols = weights.shape[1]
    grad_spec = pl.BlockSpec((EXT, 3 * GW), lambda i: (0, 0))
    rim_spec = pl.BlockSpec((HALO, 2 * HW), lambda i: (0, 0))
    return call(
        token_kernel,
        shape(ROWS, D, BF16),
        *grads,
        from_left,
        from_right,
        weights,
        vmem=24,
        grid=(D // block,),
        in_specs=[grad_spec] * 3 + [rim_spec] * 2 + [pl.BlockSpec((block, cols), lambda i: (i, 0))],
        out_specs=pl.BlockSpec((ROWS, block), lambda i: (0, i)),
        scratch_shapes=[pltpu.VMEM((ROWS, cols), BF16)],
        cost_estimate=cost(2 * ROWS * D * cols, 12_000_000),
    )


def body(tokens, weights, cotangent, token_types, incidence, window_reach):
    own = tokens[0]
    dp, loop = lax.axis_index("dp"), lax.axis_index("loop")
    place = jnp.stack([dp % 4, dp // 4 * 2 + loop // 2 % 2, loop // 4, loop % 2]).astype(jnp.int32)
    left = lax.ppermute(own[ROWS - HALO :], "loop", along_loop(1))
    right = lax.ppermute(own[:HALO], "loop", along_loop(-1))
    mask = make_mask(token_types, loop * ROWS, incidence[0], window_reach[0])
    proj = projection(own, left, right, weights)

    first = ("y", "x", "y")
    carried, grads, others, waiting = (), [], [], []

    def attend(group, after):
        nonlocal carried
        *carried, grad = attention(group, proj, cotangent[0], mask, carried, after)
        grads.append(grad)
        others.append(lax.ppermute(grad, AXES, TO_CORE))

    def weigh(group, after):
        keep, *sent = weight_parts(first[group], x_own, x_other, grads[group], others[group], after)
        waiting.append((keep, exchange(sent, ACROSS_Y if first[group] == "y" else ACROSS_X)))
        return keep

    attend(0, ())
    x_own, x_send = reorder(place, own, left, right, grads[0])
    x_other = lax.ppermute(x_send, AXES, TO_CORE)
    attend(1, (x_own,))
    keep = weigh(0, grads[1])
    attend(2, (keep,))
    keep = weigh(1, grads[2])
    weigh(2, keep)
    attended, rim_left, rim_right = carried
    from_right = lax.ppermute(rim_left, "loop", along_loop(-1))
    from_left = lax.ppermute(rim_right, "loop", along_loop(1))

    parts = []
    for group in range(GROUPS):
        keep, *sent = split_sum(*waiting[group])
        parts += [keep, *exchange(sent, ACROSS_X if first[group] == "y" else ACROSS_Y)]
    keep, send = halves(join_kernel, 24, *parts)
    keep, send = halves(halve_kernel, 12, keep, lax.ppermute(send, AXES, ACROSS_Z[0]))
    keep, send = halves(halve_kernel, 6, keep, lax.ppermute(send, AXES, ACROSS_Z[1]))
    weight_grad = call(
        functools.partial(last_kernel, (256 * ROWS) ** -0.5),
        shape(6, 3 * HW, F32),
        keep,
        lax.ppermute(send, AXES, ACROSS_Z[2]),
        in_specs=[whole()] * 2,
        out_specs=whole(),
    )
    token_grad = token_gradient(grads, from_left, from_right, weights)
    return attended[None], token_grad[None], weight_grad


def solution(mesh):
    in_specs = (
        P("dp", "loop", None),
        P(),
        P("dp", "loop", None),
        P("dp", None),
        P("dp", "loop", None),
        P("dp", "loop"),
    )
    out_specs = (P("dp", "loop", None), P("dp", "loop", None), P(("dp", "loop"), None))
    return jax.shard_map(body, mesh=mesh, in_specs=in_specs, out_specs=out_specs, check_vma=False)
```

```python
import functools

import jax
import jax.numpy as jnp
from jax import lax
from jax.experimental import pallas as pl
from jax.experimental.pallas import tpu as pltpu
from jax.sharding import PartitionSpec as P

HEADS = 12
HD = 64
TILE = 64
CAP = 20
HW = 768
HALO = 64
GROUPS = 3
GW = HW // GROUPS
GH = HEADS // GROUPS
ROWS = 512
EXT = ROWS + 2 * HALO
TILES = ROWS // TILE
WIN = 3 * TILE
D = 1536
HALF = D // 2
AXES = ("dp", "loop")
MIB = 1024 * 1024
F32 = jnp.float32
BF16 = jnp.bfloat16

NT = (((1,), (1,)), ((), ()))
TN = (((0,), (0,)), ((), ()))
NN = (((1,), (0,)), ((), ()))


def dot(a, b, dims):
    return lax.dot_general(a, b, dims, preferred_element_type=F32)


def device_at(x, y, z, core):
    return (((y // 2 * 4 + x) * 8 + z) * 2 + y % 2) * 2 + core


def route(move):
    pairs = []
    for x in range(4):
        for y in range(4):
            for z in range(8):
                for core in range(2):
                    pairs.append((device_at(x, y, z, core), device_at(*move(x, y, z, core))))
    return pairs


TO_CORE = route(lambda x, y, z, c: (x, y, z, 1 - c))
ACROSS_X = [route(lambda x, y, z, c, m=m: (x ^ m, y, z, c)) for m in (1, 2, 3)]
ACROSS_Y = [route(lambda x, y, z, c, m=m: (x, y ^ m, z, c)) for m in (1, 2, 3)]
ACROSS_Z = {m: route(lambda x, y, z, c, m=m: (x, y, z ^ m, c)) for m in (1, 2, 3, 4)}


def along_loop(distance):
    return [((i - distance) % 32, i) for i in range(32)]


def call(kernel, out_shape, *args, vmem=16, estimate=None, **kwargs):
    return pl.pallas_call(
        kernel,
        out_shape=out_shape,
        cost_estimate=estimate or TINY,
        compiler_params=pltpu.CompilerParams(vmem_limit_bytes=vmem * MIB),
        **kwargs,
    )(*args)


def whole():
    return pl.BlockSpec(memory_space=pltpu.VMEM)


def scalars():
    return pl.BlockSpec(memory_space=pltpu.SMEM)


def anywhere():
    return pl.BlockSpec(memory_space=pl.ANY)


def shape(rows, cols, dtype):
    return jax.ShapeDtypeStruct((rows, cols), dtype)


TINY = pl.CostEstimate(flops=1000, bytes_accessed=1000, transcendentals=0)


def cost(microseconds):
    return pl.CostEstimate(flops=microseconds * 1_000_000_000, bytes_accessed=1000, transcendentals=0)


def mask_kernel(incidence_ref, reach_ref, place_ref, types_ref, _, out_ref):
    seq_len = types_ref.shape[1]
    start = place_ref[4] * ROWS
    ahead = pl.multiple_of(lax.rem(start + seq_len - 2 * HALO, seq_len), 2 * HALO)
    behind = pl.multiple_of(lax.rem(start + ROWS, seq_len), 2 * HALO)
    before = types_ref[:, pl.ds(ahead, 2 * HALO)]
    here = types_ref[:, pl.ds(pl.multiple_of(start, ROWS), ROWS)]
    after = types_ref[:, pl.ds(behind, 2 * HALO)]
    row = jnp.concatenate([before[:, HALO:], here, after[:, :HALO]], axis=1).astype(F32)
    column = jnp.broadcast_to(row, (2 * TILE, EXT)).T
    key = lax.broadcasted_iota(jnp.int32, (WIN, 2 * TILE), 0)
    query = lax.broadcasted_iota(jnp.int32, (WIN, 2 * TILE), 1) % TILE
    distance = jnp.abs(key - HALO - query)
    for t in range(TILES):
        own = row[:, HALO + t * TILE : HALO + (t + 1) * TILE]
        other_kind = column[t * TILE : t * TILE + WIN] != jnp.concatenate([own, own], axis=1)
        linked = [jnp.full((TILE, 2 * TILE), incidence_ref[r, t], jnp.int32) for r in range(3)]
        linked = jnp.concatenate(linked, axis=0) == 1
        allowed = (distance == 0) | ((distance <= reach_ref[t]) & other_kind & linked)
        out_ref[t * WIN : (t + 1) * WIN, :] = jnp.where(allowed, 1.0, 0.0)


def make_mask(types, place, incidence, reach, after):
    return call(
        mask_kernel,
        shape(TILES * WIN, 2 * TILE, F32),
        incidence.T,
        reach,
        place,
        types,
        after,
        estimate=cost(2),
        in_specs=[scalars(), scalars(), scalars(), whole(), anywhere()],
        out_specs=whole(),
    )


def projection_kernel(own_ref, left_ref, right_ref, w_ref, _, out_ref, rows):
    @pl.when(pl.program_id(0) == 0)
    def _():
        rows[:ROWS] = own_ref[...]
        rows[ROWS : ROWS + HALO] = left_ref[...]
        rows[ROWS + HALO :] = right_ref[...]

    out_ref[...] = dot(rows[...], w_ref[...], NN).astype(BF16)


def projection(own, left, right, weights, after):
    cols = weights.shape[1]
    return call(
        projection_kernel,
        shape(EXT, cols, BF16),
        own,
        left,
        right,
        weights,
        after,
        vmem=32,
        grid=(3,),
        in_specs=[
            pl.BlockSpec((ROWS, D), lambda i: (0, 0)),
            pl.BlockSpec((HALO, D), lambda i: (0, 0)),
            pl.BlockSpec((HALO, D), lambda i: (0, 0)),
            pl.BlockSpec((D, HW), lambda i: (0, i)),
            anywhere(),
        ],
        out_specs=pl.BlockSpec((EXT, HW), lambda i: (0, i)),
        scratch_shapes=[pltpu.VMEM((EXT, D), BF16)],
    )


def reorder_kernel(n_carried, place_ref, rows, *refs):
    same_ref, other_ref, mark_ref = refs[n_carried:]
    mark_ref[...] = jnp.zeros_like(mark_ref)
    x, y, z, core = place_ref[0], place_ref[1], place_ref[2], place_ref[3]
    block = D // 4
    half = block // 2
    place = lax.broadcasted_iota(jnp.int32, (block, block), 0)
    feature = lax.broadcasted_iota(jnp.int32, (block, block), 1)
    other = (place >= half).astype(jnp.int32)
    place = place - other * half
    low_y = (place >= half // 2).astype(jnp.int32)
    place = place - low_y * (half // 2)
    low_x = (place >= half // 4).astype(jnp.int32)
    place = place - low_x * (half // 4)
    spot = lax.shift_right_logical(place * 10923, 16)
    place = place - spot * 6
    to_z = z ^ (lax.shift_right_logical(spot, 2) + (spot & 2) + (spot & 1) * 4)
    source = (low_x ^ (x & 1)) * half + to_z * 24 + (low_y ^ (y & 1)) * 12 + (other ^ core) * 6 + place
    pick = jnp.where(feature == source, 1.0, 0.0).astype(BF16)
    piece = half // 4
    for a in range(2):
        for b in range(2):
            at = (lax.shift_right_logical(y, 1) ^ a) * 2 + (lax.shift_right_logical(x, 1) ^ b)
            cols = rows[:, pl.ds(pl.multiple_of(at * block, 128), block)]
            got = dot(pick, cols, NT).astype(BF16)
            for c, ref in enumerate((same_ref, other_ref)):
                for low in range(4):
                    jy, jx = 2 * a + low // 2, 2 * b + low % 2
                    ref[jy * half + jx * piece : jy * half + (jx + 1) * piece] = got[
                        c * half + low * piece : c * half + (low + 1) * piece
                    ]


def reorder(place, rows, at, carried, after):
    n_rows = rows.shape[0]
    out_spec = pl.BlockSpec((HALF, n_rows), lambda i: (0, at // n_rows))
    extra = list(carried) + list(after)
    return call(
        functools.partial(reorder_kernel, len(extra)),
        (shape(HALF, EXT, BF16),) * 2 + (shape(8, 128, F32),),
        place,
        rows,
        *extra,
        estimate=cost(4),
        grid=(1,),
        in_specs=[scalars(), pl.BlockSpec((n_rows, D), lambda i: (0, 0))] + [anywhere()] * len(extra),
        out_specs=(out_spec,) * 2 + (whole(),),
        input_output_aliases={2 + i: i for i in range(len(carried))},
    )


def attention_kernel(n_carried, q_ref, k_ref, v_ref, go_ref, mask_ref, *refs):
    att_ref, left_ref, right_ref, grad_ref, ke, ve, dk, dv = refs[n_carried:]
    for src, dst in ((k_ref, ke), (v_ref, ve)):
        dst[:HALO] = src[ROWS : ROWS + HALO]
        dst[HALO : HALO + ROWS] = src[:ROWS]
        dst[HALO + ROWS :] = src[ROWS + HALO :]
    dk[...] = jnp.zeros_like(dk)
    dv[...] = jnp.zeros_like(dv)
    head_of_lane = lax.broadcasted_iota(jnp.int32, (TILE, GW), 1) // HD

    def spread(rows):
        zero = jnp.zeros_like(rows)
        return jnp.concatenate([jnp.where(head_of_lane == h, rows, zero) for h in range(GH)], axis=0)

    def gather(square):
        out = square[:TILE]
        for h in range(1, GH):
            out = jnp.where(head_of_lane == h, square[h * TILE : (h + 1) * TILE], out)
        return out

    def step(t, _):
        at = pl.multiple_of(t * TILE, TILE)
        rows = pl.ds(at, TILE)
        window = pl.ds(at, WIN)
        q_bd = spread(q_ref[rows, :])
        g_bd = spread(go_ref[rows, :])
        k_win = ke[window, :]
        v_win = ve[window, :]
        mask = mask_ref[pl.ds(pl.multiple_of(t * WIN, WIN), WIN), :]
        mask = jnp.concatenate([mask] * (GH // 2), axis=1)
        bent = jnp.tanh(dot(k_win, q_bd, NT) * (HD**-0.5 / CAP))
        numer = jnp.exp(bent * CAP) * mask
        probs = numer * (1.0 / jnp.sum(numer, axis=0, keepdims=True))
        low = probs.astype(BF16)
        weighted = probs * dot(v_win, g_bd, NT)
        delta = jnp.sum(weighted, axis=0, keepdims=True)
        scores = ((weighted - probs * delta) * (1.0 - bent * bent)).astype(BF16)
        dk[window, :] += dot(scores, q_bd, NN)
        dv[window, :] += dot(low, g_bd, NN)
        att_ref[rows, :] = gather(dot(low, v_win, TN)).astype(BF16)
        grad_ref[rows, :GW] = (gather(dot(scores, k_win, TN)) * HD**-0.5).astype(BF16)
        return 0

    lax.fori_loop(0, TILES, step, 0, unroll=True)
    grad_ref[ROWS:, :GW] = jnp.zeros((2 * HALO, GW), BF16)
    for part, acc, factor in ((1, dk, HD**-0.5), (2, dv, 1.0)):
        cols = slice(part * GW, (part + 1) * GW)
        rim_cols = slice((part - 1) * GW, part * GW)
        left = (acc[:HALO] * factor).astype(BF16)
        right = (acc[HALO + ROWS :] * factor).astype(BF16)
        grad_ref[:ROWS, cols] = (acc[HALO : HALO + ROWS] * factor).astype(BF16)
        grad_ref[ROWS : ROWS + HALO, cols] = left
        grad_ref[ROWS + HALO :, cols] = right
        left_ref[:, rim_cols] = left
        right_ref[:, rim_cols] = right


def attention(group, proj, grad_out, mask, carried, after):
    def cols(rows, block, width=GW):
        return pl.BlockSpec((rows, width), lambda i: (0, block))

    extra = list(carried) + list(after)
    return call(
        functools.partial(attention_kernel, len(extra)),
        (shape(ROWS, HW, BF16), shape(HALO, 2 * HW, BF16), shape(HALO, 2 * HW, BF16), shape(EXT, 3 * GW, BF16)),
        proj,
        proj,
        proj,
        grad_out,
        mask,
        *extra,
        vmem=20,
        grid=(1,),
        in_specs=[
            cols(ROWS, group),
            cols(EXT, GROUPS + group),
            cols(EXT, 2 * GROUPS + group),
            cols(ROWS, group),
            pl.BlockSpec((TILES * WIN, 2 * TILE), lambda i: (0, 0)),
        ]
        + [anywhere()] * len(extra),
        out_specs=(
            cols(ROWS, group),
            cols(HALO, group, 2 * GW),
            cols(HALO, group, 2 * GW),
            pl.BlockSpec((EXT, 3 * GW), lambda i: (0, 0)),
        ),
        scratch_shapes=[
            pltpu.VMEM((EXT, GW), BF16),
            pltpu.VMEM((EXT, GW), BF16),
            pltpu.VMEM((EXT, GW), F32),
            pltpu.VMEM((EXT, GW), F32),
        ],
        input_output_aliases={5 + i: i for i in range(len(carried))},
    )


SENT = (((0, 3), (1, 2)), ((0, 1), (3, 2)))


def weight_kernel(first, chosen, n_grads, x_ref, xp_ref, *refs):
    part = HALF // 4
    piece = part // 4
    outs = refs[-4:]
    for n, (g, block) in enumerate(chosen):
        cols = slice(block * GW, (block + 1) * GW)
        total = dot(x_ref[...], refs[g][:, cols], NN) + dot(xp_ref[...], refs[n_grads + g][:, cols], NN)
        cols = slice(n * GW, (n + 1) * GW)
        for half, picked in enumerate(SENT):
            for ref, parts in zip(outs[2 * half : 2 * half + 2], picked):
                for m, j in enumerate(parts):
                    for i in range(2):
                        jy, jx = (j, 2 * half + i) if first == "y" else (2 * half + i, j)
                        rows = total[jy * part + jx * piece : jy * part + (jx + 1) * piece]
                        ref[(2 * m + i) * piece : (2 * m + i + 1) * piece, cols] = rows.astype(ref.dtype)


def weight_parts(first, chosen, x_own, x_other, grads, others, after):
    rows, cols = HALF // 4, GW * len(chosen)
    n_in = 2 + 2 * len(grads)
    return call(
        functools.partial(weight_kernel, first, chosen, len(grads)),
        (shape(rows, cols, F32), shape(rows, cols, BF16)) * 2,
        x_own,
        x_other,
        *grads,
        *others,
        *after,
        vmem=24,
        in_specs=[whole()] * n_in + [anywhere()] * len(after),
        out_specs=(whole(),) * 4,
    )


def middle_kernel(a_ref, got_a_ref, b_ref, got_b_ref, *refs):
    for n, (ref, got) in enumerate(((a_ref, got_a_ref), (b_ref, got_b_ref))):
        keep_ref, send_ref = refs[2 * n - 4], refs[2 * n - 3]
        half = keep_ref.shape[0]
        total = ref[...] + got[...].astype(F32)
        keep_ref[...] = total[:half]
        send_ref[...] = total[half:].astype(BF16)


def middle(keep_a, got_a, keep_b, got_b, after):
    rows, cols = keep_a.shape[0] // 2, keep_a.shape[1]
    return call(
        middle_kernel,
        (shape(rows, cols, F32), shape(rows, cols, BF16)) * 2,
        keep_a,
        got_a,
        keep_b,
        got_b,
        *after,
        in_specs=[whole()] * 4 + [anywhere()] * len(after),
        out_specs=(whole(),) * 4,
    )


def split_kernel(a_ref, got_a_ref, b_ref, got_b_ref, *refs):
    out_ref, *send_refs = refs[-4:]
    part = out_ref.shape[0]
    for j in range(4):
        ref, got = ((a_ref, got_a_ref), (b_ref, got_b_ref))[j // 2]
        rows = slice(j % 2 * part, (j % 2 + 1) * part)
        total = ref[rows] + got[rows].astype(F32)
        if j == 0:
            out_ref[...] = total
        else:
            send_refs[j - 1][...] = total.astype(BF16)


def split_sum(keep_a, got_a, keep_b, got_b, after):
    rows, cols = keep_a.shape[0] // 2, keep_a.shape[1]
    return call(
        split_kernel,
        (shape(rows, cols, F32),) + (shape(rows, cols, BF16),) * 3,
        keep_a,
        got_a,
        keep_b,
        got_b,
        *after,
        in_specs=[whole()] * 4 + [anywhere()] * len(after),
        out_specs=(whole(),) * 4,
    )


def join_kernel(*refs):
    keep_ref, *send_refs = refs[-4:]
    at = 0
    for n in range(0, len(refs) - 4, 4):
        total = refs[n][...]
        for r in refs[n + 1 : n + 4]:
            total = total + r[...].astype(F32)
        cols = slice(at, at + total.shape[1])
        at += total.shape[1]
        part = keep_ref.shape[0]
        keep_ref[:, cols] = total[:part]
        for j in range(3):
            send_refs[j][:, cols] = total[(j + 1) * part : (j + 2) * part].astype(BF16)


def halve_kernel(keep_ref, a_ref, b_ref, c_ref, out_ref, send_ref):
    half = out_ref.shape[0]
    total = keep_ref[...] + a_ref[...].astype(F32) + b_ref[...].astype(F32) + c_ref[...].astype(F32)
    out_ref[...] = total[:half]
    send_ref[...] = total[half:].astype(BF16)


def last_kernel(factor, keep_ref, got_ref, out_ref):
    total = (keep_ref[...] + got_ref[...].astype(F32)) * factor
    for g in range(GROUPS):
        for k in range(3):
            at = (g * 3 + k) * GW
            out_ref[:, k * HW + g * GW : k * HW + (g + 1) * GW] = total[:, at : at + GW]


def cut_rows(kernel, rows, n_sent, *args):
    cols = 3 * HW
    return call(
        kernel,
        (shape(rows, cols, F32),) + (shape(rows, cols, BF16),) * n_sent,
        *args,
        in_specs=[whole()] * len(args),
        out_specs=(whole(),) * (1 + n_sent),
    )


def token_kernel(a_ref, b_ref, c_ref, left_ref, right_ref, w_ref, _, out_ref, mark_ref, grad):
    @pl.when(pl.program_id(0) == 0)
    def _():
        for g, ref in enumerate((a_ref, b_ref, c_ref)):
            for k in range(3):
                cols = slice(k * HW + g * GW, k * HW + (g + 1) * GW)
                own = slice(k * GW, (k + 1) * GW)
                if k == 0:
                    grad[:, cols] = ref[:ROWS, own]
                    continue
                rim = slice((2 * g + k - 1) * GW, (2 * g + k) * GW)
                for edge, got in ((slice(0, HALO), left_ref), (slice(ROWS - HALO, ROWS), right_ref)):
                    grad[edge, cols] = (ref[edge, own].astype(F32) + got[:, rim].astype(F32)).astype(BF16)
                grad[HALO : ROWS - HALO, cols] = ref[HALO : ROWS - HALO, own]

    out_ref[...] = dot(grad[...], w_ref[...], NT).astype(BF16)
    mark_ref[...] = jnp.zeros_like(mark_ref)


def token_gradient(grads, from_left, from_right, weights, after):
    block = 512
    cols = weights.shape[1]
    grad_spec = pl.BlockSpec((EXT, 3 * GW), lambda i: (0, 0))
    rim_spec = pl.BlockSpec((HALO, 2 * HW), lambda i: (0, 0))
    return call(
        token_kernel,
        (shape(ROWS, D, BF16), shape(8, 128, F32)),
        *grads,
        from_left,
        from_right,
        weights,
        after,
        vmem=24,
        grid=(D // block,),
        in_specs=[grad_spec] * 3 + [rim_spec] * 2 + [pl.BlockSpec((block, cols), lambda i: (i, 0)), anywhere()],
        out_specs=(pl.BlockSpec((ROWS, block), lambda i: (0, i)), pl.BlockSpec((8, 128), lambda i: (0, 0))),
        scratch_shapes=[pltpu.VMEM((ROWS, cols), BF16)],
    )


def body(tokens, weights, cotangent, token_types, incidence, window_reach):
    own = tokens[0]
    dp, loop = lax.axis_index("dp"), lax.axis_index("loop")
    place = jnp.stack([dp % 4, dp // 4 * 2 + loop // 2 % 2, loop // 4, loop % 2, loop]).astype(jnp.int32)
    left = lax.ppermute(own[ROWS - HALO :], "loop", along_loop(1))
    right = lax.ppermute(own[:HALO], "loop", along_loop(-1))
    *arranged, mark = reorder(place, own, 0, (), ())
    mask = make_mask(token_types, place, incidence[0], window_reach[0], mark)
    x_own, x_send, mark = reorder(place, jnp.concatenate([left, right], axis=0), ROWS, arranged, (mask,))
    x_other = lax.ppermute(x_send, AXES, TO_CORE)
    proj = projection(own, left, right, weights, mark)

    blocks = [(g, k) for g in range(GROUPS) for k in range(3)]
    carried, grads, others = (), [], []

    def attend(group, after):
        nonlocal carried
        *carried, grad = attention(group, proj, cotangent[0], mask, carried, after)
        grads.append(grad)
        others.append(lax.ppermute(grad, AXES, TO_CORE))

    def swap(n, way, part):
        return lax.ppermute(part, AXES, (ACROSS_Y if way == "y" else ACROSS_X)[n - 1])

    def round_one(way, chosen, after):
        used = sorted({g for g, _ in chosen})
        chosen = tuple((used.index(g), k) for g, k in chosen)
        mine, theirs = [grads[g] for g in used], [others[g] for g in used]
        keep_a, send_a, keep_b, send_b = weight_parts(way, chosen, x_own, x_other, mine, theirs, after)
        return keep_a, swap(1, way, send_a), keep_b, swap(3, way, send_b)

    def round_two(way, state, after):
        keep_a, send_a, keep_b, send_b = middle(*state, after)
        return keep_a, swap(3, way, send_a), keep_b, swap(1, way, send_b)

    def round_three(way, state, after):
        keep, *sent = split_sum(*state, after)
        return [keep, *(swap(n + 1, way, part) for n, part in enumerate(sent))]

    attend(0, ())
    attend(1, ())
    attend(2, ())
    attended, rim_left, rim_right = carried
    from_right = lax.ppermute(rim_left, "loop", along_loop(-1))
    from_left = lax.ppermute(rim_right, "loop", along_loop(1))
    by_y = round_one("y", blocks[:5], (rim_left,))
    by_x = round_one("x", blocks[5:], (by_y[0], from_left, from_right))
    token_grad, mark = token_gradient(grads, from_left, from_right, weights, by_x[0])
    by_y = round_two("y", by_y, (mark,))
    by_x = round_two("x", by_x, (by_y[0],))
    by_y = round_three("x", by_y, (by_x[0],))
    by_x = round_three("y", by_x, (by_y[0],))
    keep, *sent = cut_rows(join_kernel, 12, 3, *by_y, *by_x)
    got = [lax.ppermute(part, AXES, ACROSS_Z[m]) for part, m in zip(sent, (2, 1, 3))]
    keep, send = cut_rows(halve_kernel, 6, 1, keep, *got)
    weight_grad = call(
        functools.partial(last_kernel, (256 * ROWS) ** -0.5),
        shape(6, 3 * HW, F32),
        keep,
        lax.ppermute(send, AXES, ACROSS_Z[4]),
        in_specs=[whole()] * 2,
        out_specs=whole(),
    )
    return attended[None], token_grad[None], weight_grad


def solution(mesh):
    in_specs = (
        P("dp", "loop", None),
        P(),
        P("dp", "loop", None),
        P("dp", None),
        P("dp", "loop", None),
        P("dp", "loop"),
    )
    out_specs = (P("dp", "loop", None), P("dp", "loop", None), P(("dp", "loop"), None))
    return jax.shard_map(body, mesh=mesh, in_specs=in_specs, out_specs=out_specs, check_vma=False)
```

```python
import functools

import jax
import jax.numpy as jnp
from jax import lax
from jax.experimental import pallas as pl
from jax.experimental.pallas import tpu as pltpu
from jax.sharding import PartitionSpec as P

HEADS = 12
HD = 64
TILE = 64
CAP = 20
HW = 768
HALO = 64
GROUPS = 3
GW = HW // GROUPS
GH = HEADS // GROUPS
ROWS = 512
EXT = ROWS + 2 * HALO
TILES = ROWS // TILE
WIN = 3 * TILE
D = 1536
HALF = D // 2
AXES = ("dp", "loop")
MIB = 1024 * 1024
F32 = jnp.float32
BF16 = jnp.bfloat16

NT = (((1,), (1,)), ((), ()))
TN = (((0,), (0,)), ((), ()))
NN = (((1,), (0,)), ((), ()))


def dot(a, b, dims):
    return lax.dot_general(a, b, dims, preferred_element_type=F32)


def device_at(x, y, z, core):
    return (((y // 2 * 4 + x) * 8 + z) * 2 + y % 2) * 2 + core


def route(move):
    pairs = []
    for x in range(4):
        for y in range(4):
            for z in range(8):
                for core in range(2):
                    pairs.append((device_at(x, y, z, core), device_at(*move(x, y, z, core))))
    return pairs


TO_CORE = route(lambda x, y, z, c: (x, y, z, 1 - c))
ACROSS_X = [route(lambda x, y, z, c, m=m: (x ^ m, y, z, c)) for m in (1, 2, 3)]
ACROSS_Y = [route(lambda x, y, z, c, m=m: (x, y ^ m, z, c)) for m in (1, 2, 3)]
ACROSS_Z = {m: route(lambda x, y, z, c, m=m: (x, y, z ^ m, c)) for m in (1, 2, 3, 4)}


def own_place():
    dp, loop = lax.axis_index("dp"), lax.axis_index("loop")
    half = lax.shift_right_logical
    return dp & 3, (half(dp, 2) << 1) + (half(loop, 1) & 1), half(loop, 2), loop & 1


def along_loop(distance):
    return [((i - distance) % 32, i) for i in range(32)]


def call(kernel, out_shape, *args, vmem=16, estimate=None, **kwargs):
    return pl.pallas_call(
        kernel,
        out_shape=out_shape,
        cost_estimate=estimate or TINY,
        compiler_params=pltpu.CompilerParams(vmem_limit_bytes=vmem * MIB),
        **kwargs,
    )(*args)


def whole():
    return pl.BlockSpec(memory_space=pltpu.VMEM)


def scalars():
    return pl.BlockSpec(memory_space=pltpu.SMEM)


def anywhere():
    return pl.BlockSpec(memory_space=pl.ANY)


def shape(rows, cols, dtype):
    return jax.ShapeDtypeStruct((rows, cols), dtype)


TINY = pl.CostEstimate(flops=1000, bytes_accessed=1000, transcendentals=0)


def cost(microseconds):
    return pl.CostEstimate(flops=microseconds * 1_000_000_000, bytes_accessed=1000, transcendentals=0)


def mask_kernel(incidence_ref, reach_ref, types_ref, out_ref):
    seq_len = types_ref.shape[1]
    start = lax.axis_index("loop") * ROWS
    ahead = pl.multiple_of(lax.rem(start + seq_len - 2 * HALO, seq_len), 2 * HALO)
    behind = pl.multiple_of(lax.rem(start + ROWS, seq_len), 2 * HALO)
    before = types_ref[:, pl.ds(ahead, 2 * HALO)]
    here = types_ref[:, pl.ds(pl.multiple_of(start, ROWS), ROWS)]
    after = types_ref[:, pl.ds(behind, 2 * HALO)]
    row = jnp.concatenate([before[:, HALO:], here, after[:, :HALO]], axis=1).astype(F32)
    column = jnp.broadcast_to(row, (2 * TILE, EXT)).T
    key = lax.broadcasted_iota(jnp.int32, (WIN, 2 * TILE), 0)
    query = lax.broadcasted_iota(jnp.int32, (WIN, 2 * TILE), 1) % TILE
    distance = jnp.abs(key - HALO - query)
    for t in range(TILES):
        own = row[:, HALO + t * TILE : HALO + (t + 1) * TILE]
        other_kind = column[t * TILE : t * TILE + WIN] != jnp.concatenate([own, own], axis=1)
        linked = [jnp.full((TILE, 2 * TILE), incidence_ref[r, t], jnp.int32) for r in range(3)]
        linked = jnp.concatenate(linked, axis=0) == 1
        allowed = (distance == 0) | ((distance <= reach_ref[t]) & other_kind & linked)
        out_ref[t * WIN : (t + 1) * WIN, :] = jnp.where(allowed, 1.0, 0.0)


def make_mask(types, incidence, reach):
    return call(
        mask_kernel,
        shape(TILES * WIN, 2 * TILE, F32),
        incidence.T,
        reach,
        types,
        estimate=cost(2),
        in_specs=[scalars(), scalars(), whole()],
        out_specs=whole(),
    )


def projection_kernel(own_ref, left_ref, right_ref, w_ref, _, out_ref, rows):
    rows[:ROWS] = own_ref[...]
    rows[ROWS : ROWS + HALO] = left_ref[...]
    rows[ROWS + HALO :] = right_ref[...]
    for n in range(3):
        cols = slice(n * HW, (n + 1) * HW)
        out_ref[:, cols] = dot(rows[...], w_ref[:, cols], NN).astype(BF16)


def projection(own, left, right, weights, after):
    return call(
        projection_kernel,
        shape(EXT, weights.shape[1], BF16),
        own,
        left,
        right,
        weights,
        after,
        vmem=32,
        in_specs=[whole()] * 4 + [anywhere()],
        out_specs=whole(),
        scratch_shapes=[pltpu.VMEM((EXT, D), BF16)],
    )


def reorder_kernel(at, n_carried, rows, *refs):
    same_ref, other_ref, mark_ref = refs[n_carried:]
    tokens = slice(at, at + rows.shape[0])
    mark_ref[...] = jnp.zeros_like(mark_ref)
    x, y, z, core = own_place()
    block = D // 4
    half = block // 2
    place = lax.broadcasted_iota(jnp.int32, (block, block), 0)
    feature = lax.broadcasted_iota(jnp.int32, (block, block), 1)
    other = (place >= half).astype(jnp.int32)
    place = place - other * half
    low_y = (place >= half // 2).astype(jnp.int32)
    place = place - low_y * (half // 2)
    low_x = (place >= half // 4).astype(jnp.int32)
    place = place - low_x * (half // 4)
    spot = lax.shift_right_logical(place * 10923, 16)
    place = place - spot * 6
    to_z = z ^ (lax.shift_right_logical(spot, 2) + (spot & 2) + (spot & 1) * 4)
    source = (low_x ^ (x & 1)) * half + to_z * 24 + (low_y ^ (y & 1)) * 12 + (other ^ core) * 6 + place
    pick = jnp.where(feature == source, 1.0, 0.0).astype(BF16)
    piece = half // 4
    for a in range(2):
        for b in range(2):
            n = (lax.shift_right_logical(y, 1) ^ a) * 2 + (lax.shift_right_logical(x, 1) ^ b)
            cols = rows[:, pl.ds(pl.multiple_of(n * block, 128), block)]
            got = dot(pick, cols, NT).astype(BF16)
            for c, ref in enumerate((same_ref, other_ref)):
                for low in range(4):
                    jy, jx = 2 * a + low // 2, 2 * b + low % 2
                    ref[jy * half + jx * piece : jy * half + (jx + 1) * piece, tokens] = got[
                        c * half + low * piece : c * half + (low + 1) * piece
                    ]


def reorder(rows, at, carried, after):
    extra = list(carried) + list(after)
    return call(
        functools.partial(reorder_kernel, at, len(extra)),
        (shape(HALF, EXT, BF16),) * 2 + (shape(8, 128, F32),),
        rows,
        *extra,
        estimate=cost(1),
        in_specs=[whole()] * (1 + len(carried)) + [anywhere()] * len(after),
        out_specs=(whole(),) * 3,
        input_output_aliases={1 + i: i for i in range(len(carried))},
    )


def attention_kernel(n_carried, q_ref, k_ref, v_ref, go_ref, mask_ref, *refs):
    att_ref, rim_ref, grad_ref, ke, ve, dk, dv = refs[n_carried:]
    edge = pl.ds(pl.multiple_of(own_place()[3] * (HALO + ROWS), HALO), HALO)
    for src, dst in ((k_ref, ke), (v_ref, ve)):
        dst[:HALO] = src[ROWS : ROWS + HALO]
        dst[HALO : HALO + ROWS] = src[:ROWS]
        dst[HALO + ROWS :] = src[ROWS + HALO :]
    dk[...] = jnp.zeros_like(dk)
    dv[...] = jnp.zeros_like(dv)
    head_of_lane = lax.broadcasted_iota(jnp.int32, (TILE, GW), 1) // HD

    def spread(rows):
        zero = jnp.zeros_like(rows)
        return jnp.concatenate([jnp.where(head_of_lane == h, rows, zero) for h in range(GH)], axis=0)

    def gather(square):
        out = square[:TILE]
        for h in range(1, GH):
            out = jnp.where(head_of_lane == h, square[h * TILE : (h + 1) * TILE], out)
        return out

    def step(t, _):
        at = pl.multiple_of(t * TILE, TILE)
        rows = pl.ds(at, TILE)
        window = pl.ds(at, WIN)
        q_bd = spread(q_ref[rows, :])
        g_bd = spread(go_ref[rows, :])
        k_win = ke[window, :]
        v_win = ve[window, :]
        mask = mask_ref[pl.ds(pl.multiple_of(t * WIN, WIN), WIN), :]
        mask = jnp.concatenate([mask] * (GH // 2), axis=1)
        bent = jnp.tanh(dot(k_win, q_bd, NT) * (HD**-0.5 / CAP))
        numer = jnp.exp(bent * CAP) * mask
        probs = numer * (1.0 / jnp.sum(numer, axis=0, keepdims=True))
        low = probs.astype(BF16)
        weighted = probs * dot(v_win, g_bd, NT)
        delta = jnp.sum(weighted, axis=0, keepdims=True)
        scores = ((weighted - probs * delta) * (1.0 - bent * bent)).astype(BF16)
        dk[window, :] += dot(scores, q_bd, NN)
        dv[window, :] += dot(low, g_bd, NN)
        att_ref[rows, :] = gather(dot(low, v_win, TN)).astype(BF16)
        grad_ref[rows, :GW] = (gather(dot(scores, k_win, TN)) * HD**-0.5).astype(BF16)
        return 0

    lax.fori_loop(0, TILES, step, 0, unroll=True)
    grad_ref[ROWS:, :GW] = jnp.zeros((2 * HALO, GW), BF16)
    for part, acc, factor in ((1, dk, HD**-0.5), (2, dv, 1.0)):
        cols = slice(part * GW, (part + 1) * GW)
        rim_cols = slice((part - 1) * GW, part * GW)
        grad_ref[:ROWS, cols] = (acc[HALO : HALO + ROWS] * factor).astype(BF16)
        grad_ref[ROWS : ROWS + HALO, cols] = (acc[:HALO] * factor).astype(BF16)
        grad_ref[ROWS + HALO :, cols] = (acc[HALO + ROWS :] * factor).astype(BF16)
        rim_ref[:, rim_cols] = (acc[edge] * factor).astype(BF16)


def attention(group, proj, grad_out, mask, carried):
    def cols(rows, block, width=GW):
        return pl.BlockSpec((rows, width), lambda i: (0, block))

    last = group == GROUPS - 1
    n_cols = 3 * GW if last else 3 * GW * (GROUPS - 1)
    return call(
        functools.partial(attention_kernel, len(carried)),
        (shape(ROWS, HW, BF16), shape(HALO, 2 * HW, BF16), shape(EXT, n_cols, BF16)),
        proj,
        proj,
        proj,
        grad_out,
        mask,
        *carried,
        vmem=20,
        grid=(1,),
        in_specs=[
            cols(ROWS, group),
            cols(EXT, GROUPS + group),
            cols(EXT, 2 * GROUPS + group),
            cols(ROWS, group),
            pl.BlockSpec((TILES * WIN, 2 * TILE), lambda i: (0, 0)),
        ]
        + [anywhere()] * len(carried),
        out_specs=(cols(ROWS, group), cols(HALO, group, 2 * GW), cols(EXT, 0 if last else group, 3 * GW)),
        scratch_shapes=[
            pltpu.VMEM((EXT, GW), BF16),
            pltpu.VMEM((EXT, GW), BF16),
            pltpu.VMEM((EXT, GW), F32),
            pltpu.VMEM((EXT, GW), F32),
        ],
        input_output_aliases={5 + i: i for i in range(len(carried))},
    )


SENT = (((0, 3), (1, 2)), ((0, 1), (3, 2)))


def weight_kernel(first, chosen, n_grads, x_ref, xp_ref, *refs):
    part = HALF // 4
    piece = part // 4
    outs = refs[-4:]
    for n, (g, block) in enumerate(chosen):
        cols = slice(block * GW, (block + 1) * GW)
        total = dot(x_ref[...], refs[g][:, cols], NN) + dot(xp_ref[...], refs[n_grads + g][:, cols], NN)
        cols = slice(n * GW, (n + 1) * GW)
        for half, picked in enumerate(SENT):
            for ref, parts in zip(outs[2 * half : 2 * half + 2], picked):
                for m, j in enumerate(parts):
                    for i in range(2):
                        jy, jx = (j, 2 * half + i) if first == "y" else (2 * half + i, j)
                        rows = total[jy * part + jx * piece : jy * part + (jx + 1) * piece]
                        ref[(2 * m + i) * piece : (2 * m + i + 1) * piece, cols] = rows.astype(ref.dtype)


def weight_parts(first, chosen, x_own, x_other, grads, others, after):
    rows, cols = HALF // 4, GW * len(chosen)
    n_in = 2 + 2 * len(grads)
    return call(
        functools.partial(weight_kernel, first, chosen, len(grads)),
        (shape(rows, cols, F32), shape(rows, cols, BF16)) * 2,
        x_own,
        x_other,
        *grads,
        *others,
        *after,
        vmem=24,
        in_specs=[whole()] * n_in + [anywhere()] * len(after),
        out_specs=(whole(),) * 4,
    )


def middle_kernel(a_ref, got_a_ref, b_ref, got_b_ref, *refs):
    for n, (ref, got) in enumerate(((a_ref, got_a_ref), (b_ref, got_b_ref))):
        keep_ref, send_ref = refs[2 * n - 4], refs[2 * n - 3]
        half = keep_ref.shape[0]
        total = ref[...] + got[...].astype(F32)
        keep_ref[...] = total[:half]
        send_ref[...] = total[half:].astype(BF16)


def middle(keep_a, got_a, keep_b, got_b, after):
    rows, cols = keep_a.shape[0] // 2, keep_a.shape[1]
    return call(
        middle_kernel,
        (shape(rows, cols, F32), shape(rows, cols, BF16)) * 2,
        keep_a,
        got_a,
        keep_b,
        got_b,
        *after,
        in_specs=[whole()] * 4 + [anywhere()] * len(after),
        out_specs=(whole(),) * 4,
    )


def split_kernel(a_ref, got_a_ref, b_ref, got_b_ref, *refs):
    out_ref, *send_refs = refs[-4:]
    part = out_ref.shape[0]
    for j in range(4):
        ref, got = ((a_ref, got_a_ref), (b_ref, got_b_ref))[j // 2]
        rows = slice(j % 2 * part, (j % 2 + 1) * part)
        total = ref[rows] + got[rows].astype(F32)
        if j == 0:
            out_ref[...] = total
        else:
            send_refs[j - 1][...] = total.astype(BF16)


def split_sum(keep_a, got_a, keep_b, got_b, after):
    rows, cols = keep_a.shape[0] // 2, keep_a.shape[1]
    return call(
        split_kernel,
        (shape(rows, cols, F32),) + (shape(rows, cols, BF16),) * 3,
        keep_a,
        got_a,
        keep_b,
        got_b,
        *after,
        in_specs=[whole()] * 4 + [anywhere()] * len(after),
        out_specs=(whole(),) * 4,
    )


def join_kernel(*refs):
    keep_ref, *send_refs = refs[-4:]
    at = 0
    for n in range(0, len(refs) - 4, 4):
        total = refs[n][...]
        for r in refs[n + 1 : n + 4]:
            total = total + r[...].astype(F32)
        cols = slice(at, at + total.shape[1])
        at += total.shape[1]
        part = keep_ref.shape[0]
        keep_ref[:, cols] = total[:part]
        for j in range(3):
            send_refs[j][:, cols] = total[(j + 1) * part : (j + 2) * part].astype(BF16)


def halve_kernel(keep_ref, a_ref, b_ref, c_ref, out_ref, send_ref):
    half = out_ref.shape[0]
    total = keep_ref[...] + a_ref[...].astype(F32) + b_ref[...].astype(F32) + c_ref[...].astype(F32)
    out_ref[...] = total[:half]
    send_ref[...] = total[half:].astype(BF16)


def last_kernel(factor, keep_ref, got_ref, out_ref):
    total = (keep_ref[...] + got_ref[...].astype(F32)) * factor
    for g in range(GROUPS):
        for k in range(3):
            at = (g * 3 + k) * GW
            out_ref[:, k * HW + g * GW : k * HW + (g + 1) * GW] = total[:, at : at + GW]


def cut_rows(kernel, rows, n_sent, *args):
    cols = 3 * HW
    return call(
        kernel,
        (shape(rows, cols, F32),) + (shape(rows, cols, BF16),) * n_sent,
        *args,
        in_specs=[whole()] * len(args),
        out_specs=(whole(),) * (1 + n_sent),
    )


def token_kernel(a_ref, b_ref, c_ref, ao_ref, bo_ref, co_ref, rim_ref, w_ref, _, out_ref, mark_ref, grad):
    @pl.when(pl.program_id(0) == 0)
    def _():
        core = own_place()[3]
        first = core == 0
        near = pl.ds(pl.multiple_of(ROWS + core * HALO, HALO), HALO)
        for g, (ref, other) in enumerate(((a_ref, ao_ref), (b_ref, bo_ref), (c_ref, co_ref))):
            for k in range(3):
                cols = slice(k * HW + g * GW, k * HW + (g + 1) * GW)
                own = slice(k * GW, (k + 1) * GW)
                if k == 0:
                    grad[:, cols] = ref[:ROWS, own]
                    continue
                far = rim_ref[:, (2 * g + k - 1) * GW : (2 * g + k) * GW].astype(F32)
                close = other[near, own].astype(F32)
                for edge, got in (
                    (slice(0, HALO), jnp.where(first, far, close)),
                    (slice(ROWS - HALO, ROWS), jnp.where(first, close, far)),
                ):
                    grad[edge, cols] = (ref[edge, own].astype(F32) + got).astype(BF16)
                grad[HALO : ROWS - HALO, cols] = ref[HALO : ROWS - HALO, own]

    out_ref[...] = dot(grad[...], w_ref[...], NT).astype(BF16)
    mark_ref[...] = jnp.zeros_like(mark_ref)


def token_gradient(grads, others, rim, weights, after):
    block = 512
    cols = weights.shape[1]
    grad_specs = [pl.BlockSpec((EXT, 3 * GW), lambda i, n=n: (0, n)) for n in (0, 1, 0)]
    rim_spec = pl.BlockSpec((HALO, 2 * HW), lambda i: (0, 0))
    pair, last = grads
    pair_other, last_other = others
    return call(
        token_kernel,
        (shape(ROWS, D, BF16), shape(8, 128, F32)),
        pair,
        pair,
        last,
        pair_other,
        pair_other,
        last_other,
        rim,
        weights,
        after,
        vmem=40,
        grid=(D // block,),
        in_specs=grad_specs * 2 + [rim_spec, pl.BlockSpec((block, cols), lambda i: (i, 0)), anywhere()],
        out_specs=(pl.BlockSpec((ROWS, block), lambda i: (0, i)), pl.BlockSpec((8, 128), lambda i: (0, 0))),
        scratch_shapes=[pltpu.VMEM((ROWS, cols), BF16)],
    )


def body(tokens, weights, cotangent, token_types, incidence, window_reach):
    own = tokens[0]
    left = lax.ppermute(own[ROWS - HALO :], "loop", along_loop(1))
    right = lax.ppermute(own[:HALO], "loop", along_loop(-1))
    mask = make_mask(token_types, incidence[0], window_reach[0])
    *arranged, mark = reorder(own, 0, (), (mask,))
    x_own, x_send, mark = reorder(jnp.concatenate([left, right], axis=0), ROWS, arranged, (mark,))
    x_other = lax.ppermute(x_send, AXES, TO_CORE)
    proj = projection(own, left, right, weights, mark)

    blocks = [(0, n) for n in range(3 * GROUPS - 3)] + [(1, n) for n in range(3)]
    attended, rim, pair = attention(0, proj, cotangent[0], mask, ())
    attended, rim, pair = attention(1, proj, cotangent[0], mask, (attended, rim, pair))
    pair_other = lax.ppermute(pair, AXES, TO_CORE)
    attended, rim, last = attention(2, proj, cotangent[0], mask, (attended, rim))
    attended_mark = rim
    last_other = lax.ppermute(last, AXES, TO_CORE)
    rim = lax.ppermute(rim, "loop", [(i, (i - 1 + i % 2 * 2) % 32) for i in range(32)])
    grads, others = (pair, last), (pair_other, last_other)

    def swap(n, way, part):
        return lax.ppermute(part, AXES, (ACROSS_Y if way == "y" else ACROSS_X)[n - 1])

    def round_one(way, chosen, after):
        used = sorted({g for g, _ in chosen})
        chosen = tuple((used.index(g), k) for g, k in chosen)
        mine, theirs = [grads[g] for g in used], [others[g] for g in used]
        keep_a, send_a, keep_b, send_b = weight_parts(way, chosen, x_own, x_other, mine, theirs, after)
        return keep_a, swap(1, way, send_a), keep_b, swap(3, way, send_b)

    def round_two(way, state, after):
        keep_a, send_a, keep_b, send_b = middle(*state, after)
        return keep_a, swap(3, way, send_a), keep_b, swap(1, way, send_b)

    def round_three(way, state, after):
        keep, *sent = split_sum(*state, after)
        return [keep, *(swap(n + 1, way, part) for n, part in enumerate(sent))]

    by_y = round_one("y", blocks[:5], (attended_mark,))
    by_x = round_one("x", blocks[5:], (by_y[0], rim))
    token_grad, mark = token_gradient(grads, others, rim, weights, by_x[0])
    by_y = round_two("y", by_y, (mark,))
    by_x = round_two("x", by_x, (by_y[0],))
    by_y = round_three("x", by_y, (by_x[0],))
    by_x = round_three("y", by_x, (by_y[0],))
    keep, *sent = cut_rows(join_kernel, 12, 3, *by_y, *by_x)
    got = [lax.ppermute(part, AXES, ACROSS_Z[m]) for part, m in zip(sent, (2, 1, 3))]
    keep, send = cut_rows(halve_kernel, 6, 1, keep, *got)
    weight_grad = call(
        functools.partial(last_kernel, (256 * ROWS) ** -0.5),
        shape(6, 3 * HW, F32),
        keep,
        lax.ppermute(send, AXES, ACROSS_Z[4]),
        in_specs=[whole()] * 2,
        out_specs=whole(),
    )
    return attended[None], token_grad[None], weight_grad


def solution(mesh):
    in_specs = (
        P("dp", "loop", None),
        P(),
        P("dp", "loop", None),
        P("dp", None),
        P("dp", "loop", None),
        P("dp", "loop"),
    )
    out_specs = (P("dp", "loop", None), P("dp", "loop", None), P(("dp", "loop"), None))
    return jax.shard_map(body, mesh=mesh, in_specs=in_specs, out_specs=out_specs, check_vma=False)
```

```python
import functools

import jax
import jax.numpy as jnp
from jax import lax
from jax.experimental import pallas as pl
from jax.experimental.pallas import tpu as pltpu
from jax.sharding import PartitionSpec as P

HEADS = 12
HD = 64
TILE = 64
CAP = 20
HW = 768
HALO = 64
GROUPS = 3
GW = HW // GROUPS
GH = HEADS // GROUPS
ROWS = 512
EXT = ROWS + 2 * HALO
TILES = ROWS // TILE
WIN = 3 * TILE
D = 1536
HALF = D // 2
AXES = ("dp", "loop")
MIB = 1024 * 1024
F32 = jnp.float32
BF16 = jnp.bfloat16

NT = (((1,), (1,)), ((), ()))
TN = (((0,), (0,)), ((), ()))
NN = (((1,), (0,)), ((), ()))


def dot(a, b, dims):
    return lax.dot_general(a, b, dims, preferred_element_type=F32)


def device_at(x, y, z, core):
    return (((y // 2 * 4 + x) * 8 + z) * 2 + y % 2) * 2 + core


def route(move):
    pairs = []
    for x in range(4):
        for y in range(4):
            for z in range(8):
                for core in range(2):
                    pairs.append((device_at(x, y, z, core), device_at(*move(x, y, z, core))))
    return pairs


TO_CORE = route(lambda x, y, z, c: (x, y, z, 1 - c))
ACROSS_X = [route(lambda x, y, z, c, m=m: (x ^ m, y, z, c)) for m in (1, 2, 3)]
ACROSS_Y = [route(lambda x, y, z, c, m=m: (x, y ^ m, z, c)) for m in (1, 2, 3)]
ACROSS_Z = {m: route(lambda x, y, z, c, m=m: (x, y, z ^ m, c)) for m in (1, 2, 3, 4)}


def own_place():
    dp, loop = lax.axis_index("dp"), lax.axis_index("loop")
    half = lax.shift_right_logical
    return dp & 3, (half(dp, 2) << 1) + (half(loop, 1) & 1), half(loop, 2), loop & 1


def along_loop(distance):
    return [((i - distance) % 32, i) for i in range(32)]


def call(kernel, out_shape, *args, vmem=16, estimate=None, **kwargs):
    return pl.pallas_call(
        kernel,
        out_shape=out_shape,
        cost_estimate=estimate or TINY,
        compiler_params=pltpu.CompilerParams(vmem_limit_bytes=vmem * MIB),
        **kwargs,
    )(*args)


def whole():
    return pl.BlockSpec(memory_space=pltpu.VMEM)


def scalars():
    return pl.BlockSpec(memory_space=pltpu.SMEM)


def anywhere():
    return pl.BlockSpec(memory_space=pl.ANY)


def shape(rows, cols, dtype):
    return jax.ShapeDtypeStruct((rows, cols), dtype)


TINY = pl.CostEstimate(flops=1000, bytes_accessed=1000, transcendentals=0)


def cost(microseconds):
    return pl.CostEstimate(flops=microseconds * 1_000_000_000, bytes_accessed=1000, transcendentals=0)


def mask_kernel(incidence_ref, reach_ref, types_ref, _, out_ref):
    seq_len = types_ref.shape[1]
    start = lax.axis_index("loop") * ROWS
    ahead = pl.multiple_of(lax.rem(start + seq_len - 2 * HALO, seq_len), 2 * HALO)
    behind = pl.multiple_of(lax.rem(start + ROWS, seq_len), 2 * HALO)
    before = types_ref[:, pl.ds(ahead, 2 * HALO)]
    here = types_ref[:, pl.ds(pl.multiple_of(start, ROWS), ROWS)]
    after = types_ref[:, pl.ds(behind, 2 * HALO)]
    row = jnp.concatenate([before[:, HALO:], here, after[:, :HALO]], axis=1).astype(F32)
    column = jnp.broadcast_to(row, (2 * TILE, EXT)).T
    key = lax.broadcasted_iota(jnp.int32, (WIN, 2 * TILE), 0)
    query = lax.broadcasted_iota(jnp.int32, (WIN, 2 * TILE), 1) % TILE
    distance = jnp.abs(key - HALO - query)
    for t in range(TILES):
        own = row[:, HALO + t * TILE : HALO + (t + 1) * TILE]
        other_kind = column[t * TILE : t * TILE + WIN] != jnp.concatenate([own, own], axis=1)
        linked = [jnp.full((TILE, 2 * TILE), incidence_ref[r, t], jnp.int32) for r in range(3)]
        linked = jnp.concatenate(linked, axis=0) == 1
        allowed = (distance == 0) | ((distance <= reach_ref[t]) & other_kind & linked)
        out_ref[t * WIN : (t + 1) * WIN, :] = jnp.where(allowed, 1.0, 0.0)


def make_mask(types, incidence, reach, after):
    return call(
        mask_kernel,
        shape(TILES * WIN, 2 * TILE, F32),
        incidence.T,
        reach,
        types,
        after,
        estimate=cost(2),
        in_specs=[scalars(), scalars(), whole(), anywhere()],
        out_specs=whole(),
    )


def projection_kernel(own_ref, left_ref, right_ref, w_ref, _, out_ref, rows):
    rows[:ROWS] = own_ref[...]
    rows[ROWS : ROWS + HALO] = left_ref[...]
    rows[ROWS + HALO :] = right_ref[...]
    for n in range(3):
        cols = slice(n * HW, (n + 1) * HW)
        out_ref[:, cols] = dot(rows[...], w_ref[:, cols], NN).astype(BF16)


def projection(own, left, right, weights, after):
    return call(
        projection_kernel,
        shape(EXT, weights.shape[1], BF16),
        own,
        left,
        right,
        weights,
        after,
        vmem=32,
        in_specs=[whole()] * 4 + [anywhere()],
        out_specs=whole(),
        scratch_shapes=[pltpu.VMEM((EXT, D), BF16)],
    )


def reorder_kernel(at, n_carried, rows, *refs):
    same_ref, other_ref, mark_ref = refs[n_carried:]
    tokens = slice(at, at + rows.shape[0])
    mark_ref[...] = jnp.zeros_like(mark_ref)
    x, y, z, core = own_place()
    block = D // 4
    half = block // 2
    place = lax.broadcasted_iota(jnp.int32, (block, block), 0)
    feature = lax.broadcasted_iota(jnp.int32, (block, block), 1)
    other = (place >= half).astype(jnp.int32)
    place = place - other * half
    low_y = (place >= half // 2).astype(jnp.int32)
    place = place - low_y * (half // 2)
    low_x = (place >= half // 4).astype(jnp.int32)
    place = place - low_x * (half // 4)
    spot = lax.shift_right_logical(place * 10923, 16)
    place = place - spot * 6
    to_z = z ^ (lax.shift_right_logical(spot, 2) + (spot & 2) + (spot & 1) * 4)
    source = (low_x ^ (x & 1)) * half + to_z * 24 + (low_y ^ (y & 1)) * 12 + (other ^ core) * 6 + place
    pick = jnp.where(feature == source, 1.0, 0.0).astype(BF16)
    piece = half // 4
    for a in range(2):
        for b in range(2):
            n = (lax.shift_right_logical(y, 1) ^ a) * 2 + (lax.shift_right_logical(x, 1) ^ b)
            cols = rows[:, pl.ds(pl.multiple_of(n * block, 128), block)]
            got = dot(pick, cols, NT).astype(BF16)
            for c, ref in enumerate((same_ref, other_ref)):
                for low in range(4):
                    jy, jx = 2 * a + low // 2, 2 * b + low % 2
                    ref[jy * half + jx * piece : jy * half + (jx + 1) * piece, tokens] = got[
                        c * half + low * piece : c * half + (low + 1) * piece
                    ]


def reorder(rows, at, carried, after):
    extra = list(carried) + list(after)
    return call(
        functools.partial(reorder_kernel, at, len(extra)),
        (shape(HALF, EXT, BF16),) * 2 + (shape(8, 128, F32),),
        rows,
        *extra,
        estimate=cost(1),
        in_specs=[whole()] * (1 + len(carried)) + [anywhere()] * len(after),
        out_specs=(whole(),) * 3,
        input_output_aliases={1 + i: i for i in range(len(carried))},
    )


def attention_kernel(n_carried, q_ref, k_ref, v_ref, go_ref, mask_ref, *refs):
    att_ref, rim_ref, grad_ref, ke, ve, dk, dv = refs[n_carried:]
    edge = pl.ds(pl.multiple_of(own_place()[3] * (HALO + ROWS), HALO), HALO)
    for src, dst in ((k_ref, ke), (v_ref, ve)):
        dst[:HALO] = src[ROWS : ROWS + HALO]
        dst[HALO : HALO + ROWS] = src[:ROWS]
        dst[HALO + ROWS :] = src[ROWS + HALO :]
    dk[...] = jnp.zeros_like(dk)
    dv[...] = jnp.zeros_like(dv)
    head_of_lane = lax.broadcasted_iota(jnp.int32, (TILE, GW), 1) // HD

    def spread(rows):
        zero = jnp.zeros_like(rows)
        return jnp.concatenate([jnp.where(head_of_lane == h, rows, zero) for h in range(GH)], axis=0)

    def gather(square):
        out = square[:TILE]
        for h in range(1, GH):
            out = jnp.where(head_of_lane == h, square[h * TILE : (h + 1) * TILE], out)
        return out

    def step(t, _):
        at = pl.multiple_of(t * TILE, TILE)
        rows = pl.ds(at, TILE)
        window = pl.ds(at, WIN)
        q_bd = spread(q_ref[rows, :])
        g_bd = spread(go_ref[rows, :])
        k_win = ke[window, :]
        v_win = ve[window, :]
        mask = mask_ref[pl.ds(pl.multiple_of(t * WIN, WIN), WIN), :]
        mask = jnp.concatenate([mask] * (GH // 2), axis=1)
        bent = jnp.tanh(dot(k_win, q_bd, NT) * (HD**-0.5 / CAP))
        numer = jnp.exp(bent * CAP) * mask
        probs = numer * (1.0 / jnp.sum(numer, axis=0, keepdims=True))
        low = probs.astype(BF16)
        weighted = probs * dot(v_win, g_bd, NT)
        delta = jnp.sum(weighted, axis=0, keepdims=True)
        scores = ((weighted - probs * delta) * (1.0 - bent * bent)).astype(BF16)
        dk[window, :] += dot(scores, q_bd, NN)
        dv[window, :] += dot(low, g_bd, NN)
        att_ref[rows, :] = gather(dot(low, v_win, TN)).astype(BF16)
        grad_ref[rows, :GW] = (gather(dot(scores, k_win, TN)) * HD**-0.5).astype(BF16)
        return 0

    lax.fori_loop(0, TILES, step, 0, unroll=True)
    grad_ref[ROWS:, :GW] = jnp.zeros((2 * HALO, GW), BF16)
    for part, acc, factor in ((1, dk, HD**-0.5), (2, dv, 1.0)):
        cols = slice(part * GW, (part + 1) * GW)
        rim_cols = slice((part - 1) * GW, part * GW)
        grad_ref[:ROWS, cols] = (acc[HALO : HALO + ROWS] * factor).astype(BF16)
        grad_ref[ROWS : ROWS + HALO, cols] = (acc[:HALO] * factor).astype(BF16)
        grad_ref[ROWS + HALO :, cols] = (acc[HALO + ROWS :] * factor).astype(BF16)
        rim_ref[:, rim_cols] = (acc[edge] * factor).astype(BF16)


def attention(group, proj, grad_out, mask, carried):
    def cols(rows, block, width=GW):
        return pl.BlockSpec((rows, width), lambda i: (0, block))

    last = group == GROUPS - 1
    n_cols = 3 * GW if last else 3 * GW * (GROUPS - 1)
    return call(
        functools.partial(attention_kernel, len(carried)),
        (shape(ROWS, HW, BF16), shape(HALO, 2 * HW, BF16), shape(EXT, n_cols, BF16)),
        proj,
        proj,
        proj,
        grad_out,
        mask,
        *carried,
        vmem=20,
        grid=(1,),
        in_specs=[
            cols(ROWS, group),
            cols(EXT, GROUPS + group),
            cols(EXT, 2 * GROUPS + group),
            cols(ROWS, group),
            pl.BlockSpec((TILES * WIN, 2 * TILE), lambda i: (0, 0)),
        ]
        + [anywhere()] * len(carried),
        out_specs=(cols(ROWS, group), cols(HALO, group, 2 * GW), cols(EXT, 0 if last else group, 3 * GW)),
        scratch_shapes=[
            pltpu.VMEM((EXT, GW), BF16),
            pltpu.VMEM((EXT, GW), BF16),
            pltpu.VMEM((EXT, GW), F32),
            pltpu.VMEM((EXT, GW), F32),
        ],
        input_output_aliases={5 + i: i for i in range(len(carried))},
    )


SENT = (((0, 3), (1, 2)), ((0, 1), (3, 2)))


def weight_kernel(first, chosen, n_grads, x_ref, xp_ref, *refs):
    part = HALF // 4
    piece = part // 4
    outs = refs[-4:]
    for n, (g, block) in enumerate(chosen):
        cols = slice(block * GW, (block + 1) * GW)
        total = dot(x_ref[...], refs[g][:, cols], NN) + dot(xp_ref[...], refs[n_grads + g][:, cols], NN)
        cols = slice(n * GW, (n + 1) * GW)
        for half, picked in enumerate(SENT):
            for ref, parts in zip(outs[2 * half : 2 * half + 2], picked):
                for m, j in enumerate(parts):
                    for i in range(2):
                        jy, jx = (j, 2 * half + i) if first == "y" else (2 * half + i, j)
                        rows = total[jy * part + jx * piece : jy * part + (jx + 1) * piece]
                        ref[(2 * m + i) * piece : (2 * m + i + 1) * piece, cols] = rows.astype(ref.dtype)


def weight_parts(first, chosen, x_own, x_other, grads, others, after):
    rows, cols = HALF // 4, GW * len(chosen)
    n_in = 2 + 2 * len(grads)
    return call(
        functools.partial(weight_kernel, first, chosen, len(grads)),
        (shape(rows, cols, F32), shape(rows, cols, BF16)) * 2,
        x_own,
        x_other,
        *grads,
        *others,
        *after,
        vmem=24,
        in_specs=[whole()] * n_in + [anywhere()] * len(after),
        out_specs=(whole(),) * 4,
    )


def middle_kernel(a_ref, got_a_ref, b_ref, got_b_ref, *refs):
    for n, (ref, got) in enumerate(((a_ref, got_a_ref), (b_ref, got_b_ref))):
        keep_ref, send_ref = refs[2 * n - 4], refs[2 * n - 3]
        half = keep_ref.shape[0]
        total = ref[...] + got[...].astype(F32)
        keep_ref[...] = total[:half]
        send_ref[...] = total[half:].astype(BF16)


def middle(keep_a, got_a, keep_b, got_b, after):
    rows, cols = keep_a.shape[0] // 2, keep_a.shape[1]
    return call(
        middle_kernel,
        (shape(rows, cols, F32), shape(rows, cols, BF16)) * 2,
        keep_a,
        got_a,
        keep_b,
        got_b,
        *after,
        in_specs=[whole()] * 4 + [anywhere()] * len(after),
        out_specs=(whole(),) * 4,
    )


def split_kernel(a_ref, got_a_ref, b_ref, got_b_ref, *refs):
    out_ref, *send_refs = refs[-4:]
    part = out_ref.shape[0]
    for j in range(4):
        ref, got = ((a_ref, got_a_ref), (b_ref, got_b_ref))[j // 2]
        rows = slice(j % 2 * part, (j % 2 + 1) * part)
        total = ref[rows] + got[rows].astype(F32)
        if j == 0:
            out_ref[...] = total
        else:
            send_refs[j - 1][...] = total.astype(BF16)


def split_sum(keep_a, got_a, keep_b, got_b, after):
    rows, cols = keep_a.shape[0] // 2, keep_a.shape[1]
    return call(
        split_kernel,
        (shape(rows, cols, F32),) + (shape(rows, cols, BF16),) * 3,
        keep_a,
        got_a,
        keep_b,
        got_b,
        *after,
        in_specs=[whole()] * 4 + [anywhere()] * len(after),
        out_specs=(whole(),) * 4,
    )


def join_kernel(*refs):
    keep_ref, *send_refs = refs[-4:]
    at = 0
    for n in range(0, len(refs) - 4, 4):
        total = refs[n][...]
        for r in refs[n + 1 : n + 4]:
            total = total + r[...].astype(F32)
        cols = slice(at, at + total.shape[1])
        at += total.shape[1]
        part = keep_ref.shape[0]
        keep_ref[:, cols] = total[:part]
        for j in range(3):
            send_refs[j][:, cols] = total[(j + 1) * part : (j + 2) * part].astype(BF16)


def halve_kernel(keep_ref, a_ref, b_ref, c_ref, out_ref, send_ref):
    half = out_ref.shape[0]
    total = keep_ref[...] + a_ref[...].astype(F32) + b_ref[...].astype(F32) + c_ref[...].astype(F32)
    out_ref[...] = total[:half]
    send_ref[...] = total[half:].astype(BF16)


def last_kernel(factor, keep_ref, got_ref, out_ref):
    total = (keep_ref[...] + got_ref[...].astype(F32)) * factor
    for g in range(GROUPS):
        for k in range(3):
            at = (g * 3 + k) * GW
            out_ref[:, k * HW + g * GW : k * HW + (g + 1) * GW] = total[:, at : at + GW]


def cut_rows(kernel, rows, n_sent, *args):
    cols = 3 * HW
    return call(
        kernel,
        (shape(rows, cols, F32),) + (shape(rows, cols, BF16),) * n_sent,
        *args,
        in_specs=[whole()] * len(args),
        out_specs=(whole(),) * (1 + n_sent),
    )


def token_kernel(a_ref, b_ref, c_ref, ao_ref, bo_ref, co_ref, rim_ref, w_ref, _, out_ref, mark_ref, grad):
    @pl.when(pl.program_id(0) == 0)
    def _():
        core = own_place()[3]
        first = core == 0
        near = pl.ds(pl.multiple_of(ROWS + core * HALO, HALO), HALO)
        for g, (ref, other) in enumerate(((a_ref, ao_ref), (b_ref, bo_ref), (c_ref, co_ref))):
            for k in range(3):
                cols = slice(k * HW + g * GW, k * HW + (g + 1) * GW)
                own = slice(k * GW, (k + 1) * GW)
                if k == 0:
                    grad[:, cols] = ref[:ROWS, own]
                    continue
                far = rim_ref[:, (2 * g + k - 1) * GW : (2 * g + k) * GW].astype(F32)
                close = other[near, own].astype(F32)
                for edge, got in (
                    (slice(0, HALO), jnp.where(first, far, close)),
                    (slice(ROWS - HALO, ROWS), jnp.where(first, close, far)),
                ):
                    grad[edge, cols] = (ref[edge, own].astype(F32) + got).astype(BF16)
                grad[HALO : ROWS - HALO, cols] = ref[HALO : ROWS - HALO, own]

    out_ref[...] = dot(grad[...], w_ref[...], NT).astype(BF16)
    mark_ref[...] = jnp.zeros_like(mark_ref)


def token_gradient(grads, others, rim, weights, after):
    block = 512
    cols = weights.shape[1]
    grad_specs = [pl.BlockSpec((EXT, 3 * GW), lambda i, n=n: (0, n)) for n in (0, 1, 0)]
    rim_spec = pl.BlockSpec((HALO, 2 * HW), lambda i: (0, 0))
    pair, last = grads
    pair_other, last_other = others
    return call(
        token_kernel,
        (shape(ROWS, D, BF16), shape(8, 128, F32)),
        pair,
        pair,
        last,
        pair_other,
        pair_other,
        last_other,
        rim,
        weights,
        after,
        vmem=40,
        grid=(D // block,),
        in_specs=grad_specs * 2 + [rim_spec, pl.BlockSpec((block, cols), lambda i: (i, 0)), anywhere()],
        out_specs=(pl.BlockSpec((ROWS, block), lambda i: (0, i)), pl.BlockSpec((8, 128), lambda i: (0, 0))),
        scratch_shapes=[pltpu.VMEM((ROWS, cols), BF16)],
    )


def body(tokens, weights, cotangent, token_types, incidence, window_reach):
    own = tokens[0]
    left = lax.ppermute(own[ROWS - HALO :], "loop", along_loop(1))
    right = lax.ppermute(own[:HALO], "loop", along_loop(-1))
    *arranged, mark = reorder(own, 0, (), ())
    mask = make_mask(token_types, incidence[0], window_reach[0], mark)
    x_own, x_send, mark = reorder(jnp.concatenate([left, right], axis=0), ROWS, arranged, (mask,))
    x_other = lax.ppermute(x_send, AXES, TO_CORE)
    proj = projection(own, left, right, weights, mark)

    blocks = [(0, n) for n in range(3 * GROUPS - 3)] + [(1, n) for n in range(3)]
    attended, rim, pair = attention(0, proj, cotangent[0], mask, ())
    attended, rim, pair = attention(1, proj, cotangent[0], mask, (attended, rim, pair))
    pair_other = lax.ppermute(pair, AXES, TO_CORE)
    attended, rim, last = attention(2, proj, cotangent[0], mask, (attended, rim))
    attended_mark = rim
    last_other = lax.ppermute(last, AXES, TO_CORE)
    rim = lax.ppermute(rim, "loop", [(i, (i - 1 + i % 2 * 2) % 32) for i in range(32)])
    grads, others = (pair, last), (pair_other, last_other)

    def swap(n, way, part):
        return lax.ppermute(part, AXES, (ACROSS_Y if way == "y" else ACROSS_X)[n - 1])

    def round_one(way, chosen, after):
        used = sorted({g for g, _ in chosen})
        chosen = tuple((used.index(g), k) for g, k in chosen)
        mine, theirs = [grads[g] for g in used], [others[g] for g in used]
        keep_a, send_a, keep_b, send_b = weight_parts(way, chosen, x_own, x_other, mine, theirs, after)
        return keep_a, swap(1, way, send_a), keep_b, swap(3, way, send_b)

    def round_two(way, state, after):
        keep_a, send_a, keep_b, send_b = middle(*state, after)
        return keep_a, swap(3, way, send_a), keep_b, swap(1, way, send_b)

    def round_three(way, state, after):
        keep, *sent = split_sum(*state, after)
        return [keep, *(swap(n, way, sent[n - 1]) for n in (2, 1, 3))]

    by_y = round_one("y", blocks[:5], (attended_mark,))
    by_x = round_one("x", blocks[5:], (by_y[0], rim))
    token_grad, mark = token_gradient(grads, others, rim, weights, by_x[0])
    by_y = round_two("y", by_y, (mark,))
    by_x = round_two("x", by_x, (by_y[0],))
    by_y = round_three("x", by_y, (by_x[0],))
    by_x = round_three("y", by_x, (by_y[0],))
    keep, *sent = cut_rows(join_kernel, 12, 3, *by_y, *by_x)
    by_z = dict(zip((2, 1, 3), sent))
    got = [lax.ppermute(by_z[m], AXES, ACROSS_Z[m]) for m in (3, 2, 1)]
    keep, send = cut_rows(halve_kernel, 6, 1, keep, *got)
    weight_grad = call(
        functools.partial(last_kernel, (256 * ROWS) ** -0.5),
        shape(6, 3 * HW, F32),
        keep,
        lax.ppermute(send, AXES, ACROSS_Z[4]),
        in_specs=[whole()] * 2,
        out_specs=whole(),
    )
    return attended[None], token_grad[None], weight_grad


def solution(mesh):
    in_specs = (
        P("dp", "loop", None),
        P(),
        P("dp", "loop", None),
        P("dp", None),
        P("dp", "loop", None),
        P("dp", "loop"),
    )
    out_specs = (P("dp", "loop", None), P("dp", "loop", None), P(("dp", "loop"), None))
    return jax.shard_map(body, mesh=mesh, in_specs=in_specs, out_specs=out_specs, check_vma=False)
```

```python
import functools

import jax
import jax.numpy as jnp
from jax import lax
from jax.experimental import pallas as pl
from jax.experimental.pallas import tpu as pltpu
from jax.sharding import PartitionSpec as P

HEADS = 12
HD = 64
TILE = 64
CAP = 20
LOG2_E = 1.4426950408889634
HW = 768
HALO = 64
GROUPS = 3
GW = HW // GROUPS
GH = HEADS // GROUPS
ROWS = 512
EXT = ROWS + 2 * HALO
TILES = ROWS // TILE
WIN = 3 * TILE
D = 1536
HALF = D // 2
AXES = ("dp", "loop")
MIB = 1024 * 1024
F32 = jnp.float32
BF16 = jnp.bfloat16

NT = (((1,), (1,)), ((), ()))
TN = (((0,), (0,)), ((), ()))
NN = (((1,), (0,)), ((), ()))


def dot(a, b, dims):
    return lax.dot_general(a, b, dims, preferred_element_type=F32)


def device_at(x, y, z, core):
    return (((y // 2 * 4 + x) * 8 + z) * 2 + y % 2) * 2 + core


def route(move):
    pairs = []
    for x in range(4):
        for y in range(4):
            for z in range(8):
                for core in range(2):
                    pairs.append((device_at(x, y, z, core), device_at(*move(x, y, z, core))))
    return pairs


TO_CORE = route(lambda x, y, z, c: (x, y, z, 1 - c))
ACROSS_X = [route(lambda x, y, z, c, m=m: (x ^ m, y, z, c)) for m in (1, 2, 3)]
ACROSS_Y = [route(lambda x, y, z, c, m=m: (x, y ^ m, z, c)) for m in (1, 2, 3)]
ACROSS_Z = {m: route(lambda x, y, z, c, m=m: (x, y, z ^ m, c)) for m in (1, 2, 3, 4)}


def own_place():
    dp, loop = lax.axis_index("dp"), lax.axis_index("loop")
    half = lax.shift_right_logical
    return dp & 3, (half(dp, 2) << 1) + (half(loop, 1) & 1), half(loop, 2), loop & 1


def along_loop(distance):
    return [((i - distance) % 32, i) for i in range(32)]


def call(kernel, out_shape, *args, vmem=16, estimate=None, **kwargs):
    return pl.pallas_call(
        kernel,
        out_shape=out_shape,
        cost_estimate=estimate or TINY,
        compiler_params=pltpu.CompilerParams(vmem_limit_bytes=vmem * MIB),
        **kwargs,
    )(*args)


def whole():
    return pl.BlockSpec(memory_space=pltpu.VMEM)


def scalars():
    return pl.BlockSpec(memory_space=pltpu.SMEM)


def anywhere():
    return pl.BlockSpec(memory_space=pl.ANY)


def shape(rows, cols, dtype):
    return jax.ShapeDtypeStruct((rows, cols), dtype)


TINY = pl.CostEstimate(flops=1000, bytes_accessed=1000, transcendentals=0)


def cost(microseconds):
    return pl.CostEstimate(flops=microseconds * 1_000_000_000, bytes_accessed=1000, transcendentals=0)


def mask_kernel(incidence_ref, reach_ref, types_ref, out_ref):
    seq_len = types_ref.shape[1]
    start = lax.axis_index("loop") * ROWS
    ahead = pl.multiple_of(lax.rem(start + seq_len - 2 * HALO, seq_len), 2 * HALO)
    behind = pl.multiple_of(lax.rem(start + ROWS, seq_len), 2 * HALO)
    before = types_ref[:, pl.ds(ahead, 2 * HALO)]
    here = types_ref[:, pl.ds(pl.multiple_of(start, ROWS), ROWS)]
    after = types_ref[:, pl.ds(behind, 2 * HALO)]
    row = jnp.concatenate([before[:, HALO:], here, after[:, :HALO]], axis=1).astype(F32)
    column = jnp.broadcast_to(row, (2 * TILE, EXT)).T
    key = lax.broadcasted_iota(jnp.int32, (WIN, 2 * TILE), 0)
    query = lax.broadcasted_iota(jnp.int32, (WIN, 2 * TILE), 1) % TILE
    distance = jnp.abs(key - HALO - query)
    for t in range(TILES):
        own = row[:, HALO + t * TILE : HALO + (t + 1) * TILE]
        other_kind = column[t * TILE : t * TILE + WIN] != jnp.concatenate([own, own], axis=1)
        linked = [jnp.full((TILE, 2 * TILE), incidence_ref[r, 0, t], jnp.int32) for r in range(3)]
        linked = jnp.concatenate(linked, axis=0) == 1
        allowed = (distance == 0) | ((distance <= reach_ref[t]) & other_kind & linked)
        out_ref[t * WIN : (t + 1) * WIN, :] = jnp.where(allowed, 1.0, 0.0)


def make_mask(types, incidence, reach):
    return call(
        mask_kernel,
        shape(TILES * WIN, 2 * TILE, F32),
        incidence,
        reach,
        types,
        estimate=cost(2),
        in_specs=[scalars(), scalars(), whole()],
        out_specs=whole(),
    )


def projection_kernel(own_ref, left_ref, right_ref, w_ref, _, out_ref, rows):
    rows[:ROWS] = own_ref[...]
    rows[ROWS : ROWS + HALO] = left_ref[...]
    rows[ROWS + HALO :] = right_ref[...]
    for n in range(3):
        cols = slice(n * HW, (n + 1) * HW)
        out_ref[:, cols] = dot(rows[...], w_ref[:, cols], NN).astype(BF16)


def projection(own, left, right, weights, after):
    return call(
        projection_kernel,
        shape(EXT, weights.shape[1], BF16),
        own,
        left,
        right,
        weights,
        after,
        vmem=32,
        in_specs=[whole()] * 4 + [anywhere()],
        out_specs=whole(),
        scratch_shapes=[pltpu.VMEM((EXT, D), BF16)],
    )


def reorder_kernel(at, n_carried, rows, *refs):
    same_ref, other_ref, mark_ref = refs[n_carried:]
    tokens = slice(at, at + rows.shape[0])
    mark_ref[...] = jnp.zeros_like(mark_ref)
    x, y, z, core = own_place()
    block = D // 4
    half = block // 2
    place = lax.broadcasted_iota(jnp.int32, (block, block), 0)
    feature = lax.broadcasted_iota(jnp.int32, (block, block), 1)
    other = (place >= half).astype(jnp.int32)
    place = place - other * half
    low_y = (place >= half // 2).astype(jnp.int32)
    place = place - low_y * (half // 2)
    low_x = (place >= half // 4).astype(jnp.int32)
    place = place - low_x * (half // 4)
    spot = lax.shift_right_logical(place * 10923, 16)
    place = place - spot * 6
    to_z = z ^ (lax.shift_right_logical(spot, 2) + (spot & 2) + (spot & 1) * 4)
    source = (low_x ^ (x & 1)) * half + to_z * 24 + (low_y ^ (y & 1)) * 12 + (other ^ core) * 6 + place
    pick = jnp.where(feature == source, 1.0, 0.0).astype(BF16)
    piece = half // 4
    for a in range(2):
        for b in range(2):
            n = (lax.shift_right_logical(y, 1) ^ a) * 2 + (lax.shift_right_logical(x, 1) ^ b)
            cols = rows[:, pl.ds(pl.multiple_of(n * block, 128), block)]
            got = dot(pick, cols, NT).astype(BF16)
            for c, ref in enumerate((same_ref, other_ref)):
                for low in range(4):
                    jy, jx = 2 * a + low // 2, 2 * b + low % 2
                    ref[jy * half + jx * piece : jy * half + (jx + 1) * piece, tokens] = got[
                        c * half + low * piece : c * half + (low + 1) * piece
                    ]


def reorder(rows, at, carried, after):
    extra = list(carried) + list(after)
    return call(
        functools.partial(reorder_kernel, at, len(extra)),
        (shape(HALF, EXT, BF16),) * 2 + (shape(8, 128, F32),),
        rows,
        *extra,
        estimate=cost(1),
        in_specs=[whole()] * (1 + len(carried)) + [anywhere()] * len(after),
        out_specs=(whole(),) * 3,
        input_output_aliases={1 + i: i for i in range(len(carried))},
    )


def attention_kernel(n_carried, q_ref, k_ref, v_ref, go_ref, mask_ref, *refs):
    att_ref, rim_ref, grad_ref, ke, ve, dk, dv = refs[n_carried:]
    edge = pl.ds(pl.multiple_of(own_place()[3] * (HALO + ROWS), HALO), HALO)
    for src, dst in ((k_ref, ke), (v_ref, ve)):
        dst[:HALO] = src[ROWS : ROWS + HALO]
        dst[HALO : HALO + ROWS] = src[:ROWS]
        dst[HALO + ROWS :] = src[ROWS + HALO :]
    dk[...] = jnp.zeros_like(dk)
    dv[...] = jnp.zeros_like(dv)
    head_of_lane = lax.broadcasted_iota(jnp.int32, (TILE, GW), 1) // HD

    def spread(rows):
        zero = jnp.zeros_like(rows)
        return jnp.concatenate([jnp.where(head_of_lane == h, rows, zero) for h in range(GH)], axis=0)

    def gather(square):
        out = square[:TILE]
        for h in range(1, GH):
            out = jnp.where(head_of_lane == h, square[h * TILE : (h + 1) * TILE], out)
        return out

    def step(t, _):
        at = pl.multiple_of(t * TILE, TILE)
        rows = pl.ds(at, TILE)
        window = pl.ds(at, WIN)
        q_bd = spread(q_ref[rows, :])
        g_bd = spread(go_ref[rows, :])
        k_win = ke[window, :]
        v_win = ve[window, :]
        mask = mask_ref[pl.ds(pl.multiple_of(t * WIN, WIN), WIN), :]
        mask = jnp.concatenate([mask] * (GH // 2), axis=1)
        bent = jnp.tanh(dot(k_win, q_bd, NT) * (HD**-0.5 / CAP))
        numer = jnp.exp2(bent * (CAP * LOG2_E)) * mask
        probs = numer * (1.0 / jnp.sum(numer, axis=0, keepdims=True))
        low = probs.astype(BF16)
        weighted = probs * dot(v_win, g_bd, NT)
        delta = jnp.sum(weighted, axis=0, keepdims=True)
        scores = ((weighted - probs * delta) * (1.0 - bent * bent)).astype(BF16)
        dk[window, :] += dot(scores, q_bd, NN)
        dv[window, :] += dot(low, g_bd, NN)
        att_ref[rows, :] = gather(dot(low, v_win, TN)).astype(BF16)
        grad_ref[rows, :GW] = (gather(dot(scores, k_win, TN)) * HD**-0.5).astype(BF16)
        return 0

    lax.fori_loop(0, TILES, step, 0, unroll=True)
    grad_ref[ROWS:, :GW] = jnp.zeros((2 * HALO, GW), BF16)
    for part, acc, factor in ((1, dk, HD**-0.5), (2, dv, 1.0)):
        cols = slice(part * GW, (part + 1) * GW)
        rim_cols = slice((part - 1) * GW, part * GW)
        grad_ref[:ROWS, cols] = (acc[HALO : HALO + ROWS] * factor).astype(BF16)
        grad_ref[ROWS : ROWS + HALO, cols] = (acc[:HALO] * factor).astype(BF16)
        grad_ref[ROWS + HALO :, cols] = (acc[HALO + ROWS :] * factor).astype(BF16)
        rim_ref[:, rim_cols] = (acc[edge] * factor).astype(BF16)


def attention(group, proj, grad_out, mask, carried):
    def cols(rows, block, width=GW):
        return pl.BlockSpec((rows, width), lambda i: (0, block))

    last = group == GROUPS - 1
    n_cols = 3 * GW if last else 3 * GW * (GROUPS - 1)
    return call(
        functools.partial(attention_kernel, len(carried)),
        (shape(ROWS, HW, BF16), shape(HALO, 2 * HW, BF16), shape(EXT, n_cols, BF16)),
        proj,
        proj,
        proj,
        grad_out,
        mask,
        *carried,
        vmem=20,
        grid=(1,),
        in_specs=[
            cols(ROWS, group),
            cols(EXT, GROUPS + group),
            cols(EXT, 2 * GROUPS + group),
            cols(ROWS, group),
            pl.BlockSpec((TILES * WIN, 2 * TILE), lambda i: (0, 0)),
        ]
        + [anywhere()] * len(carried),
        out_specs=(cols(ROWS, group), cols(HALO, group, 2 * GW), cols(EXT, 0 if last else group, 3 * GW)),
        scratch_shapes=[
            pltpu.VMEM((EXT, GW), BF16),
            pltpu.VMEM((EXT, GW), BF16),
            pltpu.VMEM((EXT, GW), F32),
            pltpu.VMEM((EXT, GW), F32),
        ],
        input_output_aliases={5 + i: i for i in range(len(carried))},
    )


SENT = (((0, 3), (1, 2)), ((0, 1), (3, 2)))


def weight_kernel(first, chosen, n_grads, x_ref, xp_ref, *refs):
    part = HALF // 4
    piece = part // 4
    outs = refs[-4:]
    for n, (g, block) in enumerate(chosen):
        cols = slice(block * GW, (block + 1) * GW)
        total = dot(x_ref[...], refs[g][:, cols], NN) + dot(xp_ref[...], refs[n_grads + g][:, cols], NN)
        cols = slice(n * GW, (n + 1) * GW)
        for half, picked in enumerate(SENT):
            for ref, parts in zip(outs[2 * half : 2 * half + 2], picked):
                for m, j in enumerate(parts):
                    for i in range(2):
                        jy, jx = (j, 2 * half + i) if first == "y" else (2 * half + i, j)
                        rows = total[jy * part + jx * piece : jy * part + (jx + 1) * piece]
                        ref[(2 * m + i) * piece : (2 * m + i + 1) * piece, cols] = rows.astype(ref.dtype)


def weight_parts(first, chosen, x_own, x_other, grads, others, after):
    rows, cols = HALF // 4, GW * len(chosen)
    n_in = 2 + 2 * len(grads)
    return call(
        functools.partial(weight_kernel, first, chosen, len(grads)),
        (shape(rows, cols, F32), shape(rows, cols, BF16)) * 2,
        x_own,
        x_other,
        *grads,
        *others,
        *after,
        vmem=24,
        in_specs=[whole()] * n_in + [anywhere()] * len(after),
        out_specs=(whole(),) * 4,
    )


def middle_kernel(a_ref, got_a_ref, b_ref, got_b_ref, *refs):
    for n, (ref, got) in enumerate(((a_ref, got_a_ref), (b_ref, got_b_ref))):
        keep_ref, send_ref = refs[2 * n - 4], refs[2 * n - 3]
        half = keep_ref.shape[0]
        total = ref[...] + got[...].astype(F32)
        keep_ref[...] = total[:half]
        send_ref[...] = total[half:].astype(BF16)


def middle(keep_a, got_a, keep_b, got_b, after):
    rows, cols = keep_a.shape[0] // 2, keep_a.shape[1]
    return call(
        middle_kernel,
        (shape(rows, cols, F32), shape(rows, cols, BF16)) * 2,
        keep_a,
        got_a,
        keep_b,
        got_b,
        *after,
        in_specs=[whole()] * 4 + [anywhere()] * len(after),
        out_specs=(whole(),) * 4,
    )


def split_kernel(a_ref, got_a_ref, b_ref, got_b_ref, *refs):
    out_ref, *send_refs = refs[-4:]
    part = out_ref.shape[0]
    for j in range(4):
        ref, got = ((a_ref, got_a_ref), (b_ref, got_b_ref))[j // 2]
        rows = slice(j % 2 * part, (j % 2 + 1) * part)
        total = ref[rows] + got[rows].astype(F32)
        if j == 0:
            out_ref[...] = total
        else:
            send_refs[j - 1][...] = total.astype(BF16)


def split_sum(keep_a, got_a, keep_b, got_b, after):
    rows, cols = keep_a.shape[0] // 2, keep_a.shape[1]
    return call(
        split_kernel,
        (shape(rows, cols, F32),) + (shape(rows, cols, BF16),) * 3,
        keep_a,
        got_a,
        keep_b,
        got_b,
        *after,
        in_specs=[whole()] * 4 + [anywhere()] * len(after),
        out_specs=(whole(),) * 4,
    )


def join_kernel(*refs):
    keep_ref, *send_refs = refs[-4:]
    at = 0
    for n in range(0, len(refs) - 4, 4):
        total = refs[n][...]
        for r in refs[n + 1 : n + 4]:
            total = total + r[...].astype(F32)
        cols = slice(at, at + total.shape[1])
        at += total.shape[1]
        part = keep_ref.shape[0]
        keep_ref[:, cols] = total[:part]
        for j in range(3):
            send_refs[j][:, cols] = total[(j + 1) * part : (j + 2) * part].astype(BF16)


def halve_kernel(keep_ref, a_ref, b_ref, c_ref, out_ref, send_ref):
    half = out_ref.shape[0]
    total = keep_ref[...] + a_ref[...].astype(F32) + b_ref[...].astype(F32) + c_ref[...].astype(F32)
    out_ref[...] = total[:half]
    send_ref[...] = total[half:].astype(BF16)


def last_kernel(factor, keep_ref, got_ref, out_ref):
    total = (keep_ref[...] + got_ref[...].astype(F32)) * factor
    for g in range(GROUPS):
        for k in range(3):
            at = (g * 3 + k) * GW
            out_ref[:, k * HW + g * GW : k * HW + (g + 1) * GW] = total[:, at : at + GW]


def cut_rows(kernel, rows, n_sent, *args):
    cols = 3 * HW
    return call(
        kernel,
        (shape(rows, cols, F32),) + (shape(rows, cols, BF16),) * n_sent,
        *args,
        in_specs=[whole()] * len(args),
        out_specs=(whole(),) * (1 + n_sent),
    )


def token_kernel(a_ref, b_ref, c_ref, ao_ref, bo_ref, co_ref, rim_ref, w_ref, _, out_ref, mark_ref, grad):
    @pl.when(pl.program_id(0) == 0)
    def _():
        core = own_place()[3]
        first = core == 0
        near = pl.ds(pl.multiple_of(ROWS + core * HALO, HALO), HALO)
        for g, (ref, other) in enumerate(((a_ref, ao_ref), (b_ref, bo_ref), (c_ref, co_ref))):
            for k in range(3):
                cols = slice(k * HW + g * GW, k * HW + (g + 1) * GW)
                own = slice(k * GW, (k + 1) * GW)
                if k == 0:
                    grad[:, cols] = ref[:ROWS, own]
                    continue
                far = rim_ref[:, (2 * g + k - 1) * GW : (2 * g + k) * GW].astype(F32)
                close = other[near, own].astype(F32)
                for edge, got in (
                    (slice(0, HALO), jnp.where(first, far, close)),
                    (slice(ROWS - HALO, ROWS), jnp.where(first, close, far)),
                ):
                    grad[edge, cols] = (ref[edge, own].astype(F32) + got).astype(BF16)
                grad[HALO : ROWS - HALO, cols] = ref[HALO : ROWS - HALO, own]

    out_ref[...] = dot(grad[...], w_ref[...], NT).astype(BF16)
    mark_ref[...] = jnp.zeros_like(mark_ref)


def token_gradient(grads, others, rim, weights, after):
    block = 512
    cols = weights.shape[1]
    grad_specs = [pl.BlockSpec((EXT, 3 * GW), lambda i, n=n: (0, n)) for n in (0, 1, 0)]
    rim_spec = pl.BlockSpec((HALO, 2 * HW), lambda i: (0, 0))
    pair, last = grads
    pair_other, last_other = others
    return call(
        token_kernel,
        (shape(ROWS, D, BF16), shape(8, 128, F32)),
        pair,
        pair,
        last,
        pair_other,
        pair_other,
        last_other,
        rim,
        weights,
        after,
        vmem=40,
        grid=(D // block,),
        in_specs=grad_specs * 2 + [rim_spec, pl.BlockSpec((block, cols), lambda i: (i, 0)), anywhere()],
        out_specs=(pl.BlockSpec((ROWS, block), lambda i: (0, i)), pl.BlockSpec((8, 128), lambda i: (0, 0))),
        scratch_shapes=[pltpu.VMEM((ROWS, cols), BF16)],
    )


def body(tokens, weights, cotangent, token_types, incidence, window_reach):
    own = tokens[0]
    left = lax.ppermute(own[ROWS - HALO :], "loop", along_loop(1))
    right = lax.ppermute(own[:HALO], "loop", along_loop(-1))
    mask = make_mask(token_types, incidence.transpose(2, 0, 1), window_reach[0])
    *arranged, mark = reorder(own, 0, (), (mask,))
    x_own, x_send, mark = reorder(jnp.concatenate([left, right], axis=0), ROWS, arranged, (mark,))
    x_other = lax.ppermute(x_send, AXES, TO_CORE)
    proj = projection(own, left, right, weights, mark)

    blocks = [(0, n) for n in range(3 * GROUPS - 3)] + [(1, n) for n in range(3)]
    attended, rim, pair = attention(0, proj, cotangent[0], mask, ())
    attended, rim, pair = attention(1, proj, cotangent[0], mask, (attended, rim, pair))
    pair_other = lax.ppermute(pair, AXES, TO_CORE)
    attended, rim, last = attention(2, proj, cotangent[0], mask, (attended, rim))
    attended_mark = rim
    last_other = lax.ppermute(last, AXES, TO_CORE)
    rim = lax.ppermute(rim, "loop", [(i, (i - 1 + i % 2 * 2) % 32) for i in range(32)])
    grads, others = (pair, last), (pair_other, last_other)

    def swap(n, way, part):
        return lax.ppermute(part, AXES, (ACROSS_Y if way == "y" else ACROSS_X)[n - 1])

    def round_one(way, chosen, after):
        used = sorted({g for g, _ in chosen})
        chosen = tuple((used.index(g), k) for g, k in chosen)
        mine, theirs = [grads[g] for g in used], [others[g] for g in used]
        keep_a, send_a, keep_b, send_b = weight_parts(way, chosen, x_own, x_other, mine, theirs, after)
        return keep_a, swap(1, way, send_a), keep_b, swap(3, way, send_b)

    def round_two(way, state, after):
        keep_a, send_a, keep_b, send_b = middle(*state, after)
        return keep_a, swap(3, way, send_a), keep_b, swap(1, way, send_b)

    def round_three(way, state, after):
        keep, *sent = split_sum(*state, after)
        return [keep, *(swap(n + 1, way, part) for n, part in enumerate(sent))]

    by_y = round_one("y", blocks[:5], (attended_mark,))
    by_x = round_one("x", blocks[5:], (by_y[0], rim))
    token_grad, mark = token_gradient(grads, others, rim, weights, by_x[0])
    by_y = round_two("y", by_y, (mark,))
    by_x = round_two("x", by_x, (by_y[0],))
    by_y = round_three("x", by_y, (by_x[0],))
    by_x = round_three("y", by_x, (by_y[0],))
    keep, *sent = cut_rows(join_kernel, 12, 3, *by_y, *by_x)
    got = [lax.ppermute(part, AXES, ACROSS_Z[m]) for part, m in zip(sent, (2, 1, 3))]
    keep, send = cut_rows(halve_kernel, 6, 1, keep, *got)
    weight_grad = call(
        functools.partial(last_kernel, (256 * ROWS) ** -0.5),
        shape(6, 3 * HW, F32),
        keep,
        lax.ppermute(send, AXES, ACROSS_Z[4]),
        in_specs=[whole()] * 2,
        out_specs=whole(),
    )
    return attended[None], token_grad[None], weight_grad


def solution(mesh):
    in_specs = (
        P("dp", "loop", None),
        P(),
        P("dp", "loop", None),
        P("dp", None),
        P("dp", "loop", None),
        P("dp", "loop"),
    )
    out_specs = (P("dp", "loop", None), P("dp", "loop", None), P(("dp", "loop"), None))
    return jax.shard_map(body, mesh=mesh, in_specs=in_specs, out_specs=out_specs, check_vma=False)
```
